32 devices in a mesh: seq: 8 (over z, y), head: 4 (over x, core).
Axes of the slice: x: 2, y: 2, z: 4, core: 2. Of those that a mesh axis runs over, the one named last changes fastest.
Arguments:
- queries: bfloat16 [1024, 4096], P('seq', 'head'), may hold values from -6 to 6
- key_states: bfloat16 [1024, 4096], P('seq', 'head'), may hold values from -6 to 6
- value_states: bfloat16 [1024, 4096], P('seq', 'head'), may hold values from -6 to 6
- cotangent: bfloat16 [1024, 4096], P(('seq', 'head')), may hold values from -6 to 6
Outputs:
- attended: bfloat16 [1024, 4096], P(('seq', 'head'))
- query_gradient: bfloat16 [1024, 4096], P('seq', 'head')
- key_gradient: bfloat16 [1024, 4096], P('seq', 'head')
- value_gradient: bfloat16 [1024, 4096], P('seq', 'head')
The draws below stay inside these ranges and needn't reach their ends.
All inputs are finite; a program needn't handle non-finite values.
Results may differ from the reference program's by a relative error of at most 0.011.
Values may be sent and summed in bfloat16 or wider, within the bound.
A program may use at most 64 MiB of HBM per device.

```python
import math
import jax
import jax.numpy as jnp
from jax import lax

HEADS = 32
HEAD_DIM = 128
BLOCK = 128
LEVELS = 4
SEQ = 1024
N_SEQ = 8


def draw_queries(key, part):
    key = jax.random.fold_in(key, 1)
    shape = (BLOCK * N_SEQ, HEADS * HEAD_DIM)
    return jnp.clip(jax.random.normal(key, shape, jnp.float32), -6.0, 6.0).astype(jnp.bfloat16)


def draw_key_states(key, part):
    key = jax.random.fold_in(key, 2)
    shape = (BLOCK * N_SEQ, HEADS * HEAD_DIM)
    return jnp.clip(jax.random.normal(key, shape, jnp.float32), -6.0, 6.0).astype(jnp.bfloat16)


def block_scale(stream_key, dims, pieces, low, high):
    gain, own = 1.0, jax.random.fold_in(stream_key, 6)
    for dim, blocks in pieces:
        draws = jnp.exp(jax.random.uniform(jax.random.fold_in(own, dim), (blocks,), jnp.float32, low / len(pieces), high / len(pieces)))
        gain = gain * jnp.repeat(draws, dims[dim] // blocks).reshape([-1 if axis == dim else 1 for axis in range(len(dims))])
    return gain


def scatter_about(key, shape, width, most, pieces=(), kind=jnp.bfloat16):
    values = width * jax.random.normal(key, shape, jnp.float32)
    if pieces:
        values = values * block_scale(key, shape, pieces, -0.22, 0.18)
    return jnp.clip(values, -most, most).astype(kind)


def setup_inputs(seed: int = 0) -> dict:
    key_list = jax.random.split(jax.random.key(seed), 5)
    queries = draw_queries(jax.random.fold_in(key_list[4], 71), 0)
    key_states = draw_key_states(jax.random.fold_in(key_list[4], 71), 0)
    value_states = scatter_about(key_list[2], (SEQ, HEADS * HEAD_DIM), 1.0, 6.0, ((0, 8), (1, 4)))
    cotangent = scatter_about(key_list[3], (SEQ, HEADS * HEAD_DIM), 1.0, 6.0, ((0, 32),))
    return {"queries": queries, "key_states": key_states, "value_states": value_states, "cotangent": cotangent}


LOG_TWO = math.log(2.0)
MASKED = -1e+30

def pair_mean(values):
    row_count = values.shape[-2]
    grouped = values.astype(jnp.float32).reshape(values.shape[:-2] + (row_count // 2, 2, values.shape[-1]))
    return (0.5 * (grouped[..., 0, :] + grouped[..., 1, :])).astype(jnp.bfloat16)

def spread_rows(gradients):
    return jnp.repeat(0.5 * gradients, 2, axis=-2)

def attend_block(query_block, key_set, value_set, key_bias, cotangent_block):
    score_scale = 1.0 / math.sqrt(HEAD_DIM)
    flat = HEADS * HEAD_DIM
    query_wide = query_block.astype(jnp.float32).reshape(BLOCK, HEADS, HEAD_DIM)
    key_wide = key_set.astype(jnp.float32).reshape(-1, HEADS, HEAD_DIM)
    value_wide = value_set.astype(jnp.float32).reshape(-1, HEADS, HEAD_DIM)
    cotangent_wide = cotangent_block.astype(jnp.float32).reshape(BLOCK, HEADS, HEAD_DIM)
    scores = jnp.einsum('qhe,khe->hqk', query_wide, key_wide) * score_scale + key_bias
    highest = lax.optimization_barrier(jnp.max(scores, axis=2, keepdims=True))
    raised = jnp.exp(scores - highest)
    weights = raised / lax.optimization_barrier(jnp.sum(raised, axis=2, keepdims=True))
    weights_low = lax.optimization_barrier(weights.astype(jnp.bfloat16)).astype(jnp.float32)
    attended = jnp.einsum('hqk,khe->qhe', weights_low, value_wide).astype(jnp.bfloat16)
    weight_grad = jnp.einsum('qhe,khe->hqk', cotangent_wide, value_wide)
    row_term = lax.optimization_barrier(jnp.sum(weights * weight_grad, axis=2, keepdims=True))
    score_grad = (weights * (weight_grad - row_term) * score_scale).astype(jnp.bfloat16)
    score_grad = lax.optimization_barrier(score_grad).astype(jnp.float32)
    query_grad = jnp.einsum('hqk,khe->qhe', score_grad, key_wide).astype(jnp.bfloat16)
    key_grad = jnp.einsum('hqk,qhe->khe', score_grad, query_wide)
    value_grad = jnp.einsum('hqk,qhe->khe', weights_low, cotangent_wide)
    return (attended.reshape(BLOCK, flat), query_grad.reshape(BLOCK, flat), key_grad.reshape(-1, flat), value_grad.reshape(-1, flat))

def reference(queries, key_states, value_states, cotangent):
    flat = HEADS * HEAD_DIM
    total = BLOCK * N_SEQ
    reach = 2 ** LEVELS - 1
    half_rows = BLOCK // 2
    key_levels = [key_states]
    value_levels = [value_states]
    for level_index in range(1, LEVELS + 1):
        key_levels.append(pair_mean(key_levels[-1]))
        value_levels.append(pair_mean(value_levels[-1]))
    padded_keys = []
    padded_values = []
    for level_index in range(1, LEVELS + 1):
        margin = reach * (BLOCK >> level_index)
        padded_keys.append(jnp.pad(key_levels[level_index], ((margin, margin), (0, 0))))
        padded_values.append(jnp.pad(value_levels[level_index], ((margin, margin), (0, 0))))
    start_grads = tuple((jnp.zeros(padded_level.shape, jnp.float32) for padded_level in padded_keys))

    def step_block(carry, block_index):
        key_sums, value_sums = carry
        start = (block_index * BLOCK).astype(jnp.int32)
        query_block = lax.dynamic_slice_in_dim(queries, start, BLOCK, 0)
        cotangent_block = lax.dynamic_slice_in_dim(cotangent, start, BLOCK, 0)
        key_parts = [lax.dynamic_slice_in_dim(key_states, start, BLOCK, 0)]
        value_parts = [lax.dynamic_slice_in_dim(value_states, start, BLOCK, 0)]
        bias_parts = [jnp.zeros((BLOCK,), jnp.float32)]
        offsets = []
        for level_index in range(1, LEVELS + 1):
            tier_rows = BLOCK >> level_index
            row_block = jnp.arange(half_rows, dtype=jnp.int32) // tier_rows
            lower_first = block_index - 2 ** level_index + 1
            upper_first = block_index + 2 ** (level_index - 1)
            for first_block in (lower_first, upper_first):
                owner_block = first_block + row_block
                valid = (owner_block >= 0) & (owner_block < N_SEQ)
                row_start = ((first_block + reach) * tier_rows).astype(jnp.int32)
                key_parts.append(lax.dynamic_slice_in_dim(padded_keys[level_index - 1], row_start, half_rows, 0))
                value_parts.append(lax.dynamic_slice_in_dim(padded_values[level_index - 1], row_start, half_rows, 0))
                bias_parts.append(jnp.where(valid, level_index * LOG_TWO, MASKED).astype(jnp.float32))
                offsets.append((level_index, row_start))
        attended, query_grad, key_grad, value_grad = attend_block(query_block, jnp.concatenate(key_parts, axis=0), jnp.concatenate(value_parts, axis=0), jnp.concatenate(bias_parts), cotangent_block)
        key_sums = list(key_sums)
        value_sums = list(value_sums)
        for part_number, (level_index, row_start) in enumerate(offsets):
            first_row = BLOCK + part_number * half_rows
            for level_sums, set_grad in ((key_sums, key_grad), (value_sums, value_grad)):
                current = lax.dynamic_slice_in_dim(level_sums[level_index - 1], row_start, half_rows, 0)
                level_sums[level_index - 1] = lax.dynamic_update_slice_in_dim(level_sums[level_index - 1], current + set_grad[first_row:first_row + half_rows], row_start, 0)
        return ((tuple(key_sums), tuple(value_sums)), (attended, query_grad, key_grad[:BLOCK], value_grad[:BLOCK]))
    (key_sums, value_sums), (attended, query_grad, own_key, own_value) = lax.scan(step_block, (start_grads, start_grads), jnp.arange(N_SEQ, dtype=jnp.int32))

    def unfold(level_sums, own_rows):
        carried = None
        for level_index in range(LEVELS, 0, -1):
            tier_rows = BLOCK >> level_index
            core = level_sums[level_index - 1][reach * tier_rows:reach * tier_rows + N_SEQ * tier_rows]
            carried = core if carried is None else core + spread_rows(carried)
        return (own_rows.reshape(total, flat) + spread_rows(carried)).astype(jnp.bfloat16)
    return (attended.reshape(total, flat), query_grad.reshape(total, flat), unfold(key_sums, own_key), unfold(value_sums, own_value))
```

```python
import functools
import math

import jax
import jax.numpy as jnp
from jax import lax
from jax.experimental import pallas as pl
from jax.experimental.pallas import tpu as pltpu
from jax.sharding import PartitionSpec as P

HEAD_DIM = 128
LEVELS = 4
GROUPS = 2

LOG_TWO = math.log(2.0)
MASKED = -1e30
MESH = pl.DeviceIdType.MESH
F32 = jnp.float32
BF16 = jnp.bfloat16


def span_slots(blocks, block_rows):
    slots = []
    start = 0
    for level in range(1, LEVELS + 1):
        rows = max(16, block_rows >> level)
        distances = [d for d in range(2 ** (level - 1), 2**level) if d < blocks]
        for facing in (-1, 1):
            for distance in distances:
                slots.append((level, facing, distance, start, rows))
                start += rows
    return slots, start


def mirror(slots, slot):
    level, facing, distance = slot[:3]
    for number, other in enumerate(slots):
        if other[:3] == (level, -facing, distance):
            return number
    return None


def contract(left, right, left_dim, right_dim):
    return lax.dot_general(
        left, right, (((left_dim,), (right_dim,)), ((), ())), preferred_element_type=F32
    )


def kernel(
    blocks, heads_axis, slots, far_rows,
    q_hbm, k_hbm, v_hbm, c_hbm,
    att_out, qg_out, kg_out, vg_out,
    keyset, q_s, cot, bias, own, gsend, grecv, att_s, pyramid,
    in_sem, cot_own_sem, att_own_sem, ksend, krecv, gsem, gland, csend, crecv, asend, arecv,
):
    block_rows, width = q_s.shape
    out_rows = c_hbm.shape[0]
    span = width // GROUPS
    me = lax.axis_index("seq")
    my_head = lax.axis_index("head")
    score_scale = 1.0 / math.sqrt(HEAD_DIM)

    def target(slot):
        other = me + slot[1] * slot[2]
        return other, (other >= 0) & (other < blocks)

    def partner(step):
        return lax.rem(my_head + step, heads_axis)

    def columns(group):
        return pl.ds(group * span, span)

    def kv_copy(group, number):
        slot = slots[number]
        other = mirror(slots, slot)
        return pltpu.make_async_remote_copy(
            src_ref=pyramid[slot[0] - 1].at[:, :, columns(group)],
            dst_ref=keyset.at[:, pl.ds(block_rows + slots[other][3], slot[4]), columns(group)],
            send_sem=ksend.at[group, number],
            recv_sem=krecv.at[group, other],
            device_id={"seq": target(slot)[0]},
            device_id_type=MESH,
        )

    def grad_copy(group, number):
        slot = slots[number]
        other = mirror(slots, slot)
        return pltpu.make_async_remote_copy(
            src_ref=gsend.at[:, pl.ds(slot[3], slot[4]), columns(group)],
            dst_ref=grecv.at[:, pl.ds(slots[other][3], slot[4]), columns(group)],
            send_sem=gsem.at[group, number],
            recv_sem=gland.at[group, other],
            device_id={"seq": target(slot)[0]},
            device_id_type=MESH,
        )

    def cot_copy(group, step):
        other = partner(step)
        return pltpu.make_async_remote_copy(
            src_ref=c_hbm.at[:, pl.ds(pl.multiple_of(other * width + group * span, 128), span)],
            dst_ref=cot.at[pl.ds(pl.multiple_of(my_head * out_rows, 16), out_rows), columns(group)],
            send_sem=csend.at[group, step - 1],
            recv_sem=crecv.at[group, step - 1],
            device_id={"head": other},
            device_id_type=MESH,
        )

    def att_copy(group, step):
        other = partner(step)
        return pltpu.make_async_remote_copy(
            src_ref=att_s.at[pl.ds(pl.multiple_of(other * out_rows, 16), out_rows), columns(group)],
            dst_ref=att_out.at[:, pl.ds(pl.multiple_of(my_head * width + group * span, 128), span)],
            send_sem=asend.at[group, step - 1],
            recv_sem=arecv.at[group, step - 1],
            device_id={"head": other},
            device_id_type=MESH,
        )

    def att_own(group):
        return pltpu.make_async_copy(
            att_s.at[pl.ds(pl.multiple_of(my_head * out_rows, 16), out_rows), columns(group)],
            att_out.at[:, pl.ds(pl.multiple_of(my_head * width + group * span, 128), span)],
            att_own_sem.at[group],
        )

    barrier = pltpu.get_barrier_semaphore()
    greeted = heads_axis - 1
    for slot in slots:
        other, valid = target(slot)
        greeted = greeted + valid.astype(jnp.int32)

        @pl.when(valid)
        def _(other=other):
            pl.semaphore_signal(barrier, inc=1, device_id={"seq": other}, device_id_type=MESH)

    for step in range(1, heads_axis):
        pl.semaphore_signal(
            barrier, inc=1, device_id={"head": partner(step)}, device_id_type=MESH
        )

    own_rows = pl.ds(0, block_rows)
    load_k = pltpu.make_async_copy(k_hbm, keyset.at[0, own_rows], in_sem.at[0])
    load_v = pltpu.make_async_copy(v_hbm, keyset.at[1, own_rows], in_sem.at[1])
    load_q = pltpu.make_async_copy(q_hbm, q_s, in_sem.at[2])
    load_c = pltpu.make_async_copy(
        c_hbm.at[:, pl.ds(pl.multiple_of(my_head * width, 128), width)],
        cot.at[pl.ds(pl.multiple_of(my_head * out_rows, 16), out_rows)],
        cot_own_sem,
    )
    load_k.start()
    load_v.start()
    load_q.start()
    load_c.start()

    for slot in slots:
        level, _, _, first, rows = slot
        other, valid = target(slot)
        row = lax.broadcasted_iota(jnp.int32, (rows, block_rows), 0)
        shown = jnp.where(valid, level * LOG_TWO, MASKED).astype(F32)
        bias[pl.ds(block_rows + first, rows), :] = jnp.where(
            row < (block_rows >> level), shown, MASKED
        )

        @pl.when(jnp.logical_not(valid))
        def _(first=first, rows=rows):
            keyset[:, pl.ds(block_rows + first, rows), :] = jnp.zeros((2, rows, width), BF16)
            grecv[:, pl.ds(first, rows), :] = jnp.zeros((2, rows, width), BF16)

    bias[own_rows, :] = jnp.zeros((block_rows, block_rows), F32)

    load_k.wait()
    load_v.wait()
    for which in range(2):
        lower = keyset[which, own_rows, :]
        for level_ref in pyramid:
            rows, wide = level_ref.shape[1], lower.shape[0]
            row = lax.broadcasted_iota(jnp.int32, (rows, wide), 0)
            col = lax.broadcasted_iota(jnp.int32, (rows, wide), 1)
            pairs = jnp.where((col >> 1) == row, 0.5, 0.0).astype(BF16)
            lower = contract(pairs, lower, 1, 0).astype(BF16)
            level_ref[which] = lower

    pl.semaphore_wait(barrier, greeted)
    for group in range(GROUPS):
        for number, slot in enumerate(slots):

            @pl.when(target(slot)[1])
            def _(group=group, number=number):
                kv_copy(group, number).start()

        for step in range(1, heads_axis):
            cot_copy(group, step).start()

    load_q.wait()
    load_c.wait()
    for group in range(GROUPS):
        for step in range(1, heads_axis):
            cot_copy(group, step).wait_recv()
        for number, slot in enumerate(slots):

            @pl.when(target(slot)[1])
            def _(group=group, number=number):
                other = mirror(slots, slots[number])
                kv_copy(group, other).wait_recv()

        def head_pass(head_number, carry, group=group):
            cols = pl.ds(pl.multiple_of(group * span + head_number * HEAD_DIM, HEAD_DIM), HEAD_DIM)
            query, key, value, grad = q_s[:, cols], keyset[0, :, cols], keyset[1, :, cols], cot[:, cols]
            scores = contract(key, query, 1, 1) * score_scale + bias[...]
            raised = jnp.exp(scores - jnp.max(scores, axis=0, keepdims=True))
            weights = raised * (1.0 / jnp.sum(raised, axis=0, keepdims=True))
            weights_low = weights.astype(BF16)
            att_s[:, cols] = contract(weights_low, value, 0, 0).astype(BF16)
            weight_grad = contract(value, grad, 1, 1)
            row_term = jnp.sum(weights * weight_grad, axis=0, keepdims=True)
            score_grad = (weights * (weight_grad - row_term) * score_scale).astype(BF16)
            qg_out[:, cols] = contract(score_grad, key, 0, 0).astype(BF16)
            for which, (left, right) in enumerate(((score_grad, query), (weights_low, grad))):
                set_grad = contract(left, right, 1, 0)
                own[which, :, cols] = set_grad[:block_rows]
                gsend[which, :, cols] = set_grad[block_rows:].astype(BF16)
            return carry

        lax.fori_loop(0, span // HEAD_DIM, head_pass, 0)
        for number, slot in enumerate(slots):

            @pl.when(target(slot)[1])
            def _(group=group, number=number):
                grad_copy(group, number).start()

        for step in range(1, heads_axis):
            att_copy(group, step).start()
        att_own(group).start()

    for group in range(GROUPS):
        for number, slot in enumerate(slots):

            @pl.when(target(slot)[1])
            def _(group=group, number=number):
                other = mirror(slots, slots[number])
                grad_copy(group, other).wait_recv()

        for which, out in enumerate((kg_out, vg_out)):
            total = own[which, :, columns(group)]
            for level in range(1, LEVELS + 1):
                spans = [slot for slot in slots if slot[0] == level]
                if not spans:
                    continue
                first, rows = spans[0][3], spans[0][4]
                count = rows * len(spans)
                row = lax.broadcasted_iota(jnp.int32, (block_rows, count), 0)
                col = lax.broadcasted_iota(jnp.int32, (block_rows, count), 1)
                spread = jnp.where(
                    (row >> level) == (col & (rows - 1)), 0.5**level, 0.0
                ).astype(BF16)
                total = total + contract(
                    spread, grecv[which, pl.ds(first, count), columns(group)], 1, 0
                )
            out[:, columns(group)] = total.astype(BF16)

    for group in range(GROUPS):
        att_own(group).wait()
        for step in range(1, heads_axis):
            cot_copy(group, step).wait_send()
            att_copy(group, step).wait()
        for number, slot in enumerate(slots):

            @pl.when(target(slot)[1])
            def _(group=group, number=number):
                kv_copy(group, number).wait_send()
                grad_copy(group, number).wait_send()


def local(blocks, heads_axis, queries, key_states, value_states, cotangent):
    block_rows, width = queries.shape
    slots, far_rows = span_slots(blocks, block_rows)
    levels = sorted({slot[0] for slot in slots})
    count = len(slots)
    steps = heads_axis - 1
    dma = pltpu.SemaphoreType.DMA
    anywhere = pl.BlockSpec(memory_space=pl.ANY)
    vmem = pl.BlockSpec(memory_space=pltpu.VMEM)
    scratch = [
        pltpu.VMEM((2, block_rows + far_rows, width), BF16),
        pltpu.VMEM((block_rows, width), BF16),
        pltpu.VMEM((block_rows, width), BF16),
        pltpu.VMEM((block_rows + far_rows, block_rows), F32),
        pltpu.VMEM((2, block_rows, width), F32),
        pltpu.VMEM((2, far_rows, width), BF16),
        pltpu.VMEM((2, far_rows, width), BF16),
        pltpu.VMEM((block_rows, width), BF16),
        [pltpu.VMEM((2, max(16, block_rows >> level), width), BF16) for level in levels],
        dma((3,)),
        dma,
        dma((GROUPS,)),
        dma((GROUPS, count)),
        dma((GROUPS, count)),
        dma((GROUPS, count)),
        dma((GROUPS, count)),
        dma((GROUPS, steps)),
        dma((GROUPS, steps)),
        dma((GROUPS, steps)),
        dma((GROUPS, steps)),
    ]
    part = jax.ShapeDtypeStruct(queries.shape, BF16)
    set_rows = block_rows + far_rows
    return pl.pallas_call(
        functools.partial(kernel, blocks, heads_axis, slots, far_rows),
        out_shape=(jax.ShapeDtypeStruct(cotangent.shape, BF16), part, part, part),
        in_specs=[anywhere] * 4,
        out_specs=(anywhere, vmem, vmem, vmem),
        scratch_shapes=scratch,
        cost_estimate=pl.CostEstimate(
            flops=12 * block_rows * set_rows * width,
            bytes_accessed=16 * block_rows * width,
            transcendentals=block_rows * set_rows * width // HEAD_DIM,
        ),
        compiler_params=pltpu.CompilerParams(
            collective_id=0, has_side_effects=True, vmem_limit_bytes=48 * 2**20
        ),
    )(queries, key_states, value_states, cotangent)


def solution(mesh):
    placed = (P("seq", "head"), P("seq", "head"), P("seq", "head"), P(("seq", "head"), None))
    return jax.shard_map(
        functools.partial(local, mesh.shape["seq"], mesh.shape["head"]),
        mesh=mesh,
        in_specs=placed,
        out_specs=(P(("seq", "head"), None), P("seq", "head"), P("seq", "head"), P("seq", "head")),
        check_vma=False,
    )
```

```python
import functools
import math

import jax
import jax.numpy as jnp
from jax import lax
from jax.experimental import pallas as pl
from jax.experimental.pallas import tpu as pltpu
from jax.sharding import PartitionSpec as P

HEAD_DIM = 128
LEVELS = 4
GROUPS = 2

LOG_TWO = math.log(2.0)
MASKED = -1e30
MESH = pl.DeviceIdType.MESH
F32 = jnp.float32
BF16 = jnp.bfloat16


def span_slots(blocks, block_rows):
    slots = []
    start = 0
    for level in range(1, LEVELS + 1):
        rows = max(16, block_rows >> level)
        distances = [d for d in range(2 ** (level - 1), 2**level) if d < blocks]
        for facing in (-1, 1):
            for distance in distances:
                slots.append((level, facing, distance, start, rows))
                start += rows
    return slots, start


def mirror(slots, slot):
    level, facing, distance = slot[:3]
    for number, other in enumerate(slots):
        if other[:3] == (level, -facing, distance):
            return number
    return None


def contract(left, right, left_dim, right_dim):
    return lax.dot_general(
        left, right, (((left_dim,), (right_dim,)), ((), ())), preferred_element_type=F32
    )


def kernel(
    blocks, heads_axis, slots, far_rows,
    q_hbm, k_hbm, v_hbm, c_hbm,
    att_out, qg_out, kg_out, vg_out,
    keyset, q_s, cot, bias, own, gsend, grecv, att_s, pyramid,
    in_sem, cot_own_sem, att_own_sem, ksend, krecv, gsem, gland, csend, crecv, asend, arecv,
):
    block_rows, width = q_s.shape
    out_rows = c_hbm.shape[0]
    span = width // GROUPS
    me = lax.axis_index("seq")
    my_head = lax.axis_index("head")
    score_scale = 1.0 / math.sqrt(HEAD_DIM)

    def target(slot):
        other = me + slot[1] * slot[2]
        return other, (other >= 0) & (other < blocks)

    def partner(step):
        return lax.rem(my_head + step, heads_axis)

    def columns(group):
        return pl.ds(group * span, span)

    def kv_copy(group, number):
        slot = slots[number]
        other = mirror(slots, slot)
        return pltpu.make_async_remote_copy(
            src_ref=pyramid[slot[0] - 1].at[:, :, columns(group)],
            dst_ref=keyset.at[:, pl.ds(block_rows + slots[other][3], slot[4]), columns(group)],
            send_sem=ksend.at[group, number],
            recv_sem=krecv.at[group, other],
            device_id={"seq": target(slot)[0]},
            device_id_type=MESH,
        )

    def grad_copy(group, number):
        slot = slots[number]
        other = mirror(slots, slot)
        return pltpu.make_async_remote_copy(
            src_ref=gsend.at[:, pl.ds(slot[3], slot[4]), columns(group)],
            dst_ref=grecv.at[:, pl.ds(slots[other][3], slot[4]), columns(group)],
            send_sem=gsem.at[group, number],
            recv_sem=gland.at[group, other],
            device_id={"seq": target(slot)[0]},
            device_id_type=MESH,
        )

    def cot_copy(group, step):
        other = partner(step)
        return pltpu.make_async_remote_copy(
            src_ref=c_hbm.at[:, pl.ds(pl.multiple_of(other * width + group * span, 128), span)],
            dst_ref=cot.at[pl.ds(pl.multiple_of(my_head * out_rows, 16), out_rows), columns(group)],
            send_sem=csend.at[group, step - 1],
            recv_sem=crecv.at[group, step - 1],
            device_id={"head": other},
            device_id_type=MESH,
        )

    def att_copy(group, step):
        other = partner(step)
        return pltpu.make_async_remote_copy(
            src_ref=att_s.at[pl.ds(pl.multiple_of(other * out_rows, 16), out_rows), columns(group)],
            dst_ref=att_out.at[:, pl.ds(pl.multiple_of(my_head * width + group * span, 128), span)],
            send_sem=asend.at[group, step - 1],
            recv_sem=arecv.at[group, step - 1],
            device_id={"head": other},
            device_id_type=MESH,
        )

    def att_own(group):
        return pltpu.make_async_copy(
            att_s.at[pl.ds(pl.multiple_of(my_head * out_rows, 16), out_rows), columns(group)],
            att_out.at[:, pl.ds(pl.multiple_of(my_head * width + group * span, 128), span)],
            att_own_sem.at[group],
        )

    barrier = pltpu.get_barrier_semaphore()
    greeted = heads_axis - 1
    for slot in slots:
        other, valid = target(slot)
        greeted = greeted + valid.astype(jnp.int32)

        @pl.when(valid)
        def _(other=other):
            pl.semaphore_signal(barrier, inc=1, device_id={"seq": other}, device_id_type=MESH)

    for step in range(1, heads_axis):
        pl.semaphore_signal(
            barrier, inc=1, device_id={"head": partner(step)}, device_id_type=MESH
        )

    own_rows = pl.ds(0, block_rows)
    load_k = pltpu.make_async_copy(k_hbm, keyset.at[0, own_rows], in_sem.at[0])
    load_v = pltpu.make_async_copy(v_hbm, keyset.at[1, own_rows], in_sem.at[1])
    load_q = pltpu.make_async_copy(q_hbm, q_s, in_sem.at[2])
    load_c = pltpu.make_async_copy(
        c_hbm.at[:, pl.ds(pl.multiple_of(my_head * width, 128), width)],
        cot.at[pl.ds(pl.multiple_of(my_head * out_rows, 16), out_rows)],
        cot_own_sem,
    )
    load_k.start()
    load_v.start()
    load_q.start()
    load_c.start()

    for slot in slots:
        level, _, _, first, rows = slot
        other, valid = target(slot)
        row = lax.broadcasted_iota(jnp.int32, (rows, block_rows), 0)
        shown = jnp.where(valid, level * LOG_TWO, MASKED).astype(F32)
        bias[pl.ds(block_rows + first, rows), :] = jnp.where(
            row < (block_rows >> level), shown, MASKED
        )

        @pl.when(jnp.logical_not(valid))
        def _(first=first, rows=rows):
            keyset[:, pl.ds(block_rows + first, rows), :] = jnp.zeros((2, rows, width), BF16)
            grecv[:, pl.ds(first, rows), :] = jnp.zeros((2, rows, width), BF16)

    bias[own_rows, :] = jnp.zeros((block_rows, block_rows), F32)

    load_k.wait()
    load_v.wait()
    for which in range(2):
        lower = keyset[which, own_rows, :]
        for level_ref in pyramid:
            rows, wide = level_ref.shape[1], lower.shape[0]
            row = lax.broadcasted_iota(jnp.int32, (rows, wide), 0)
            col = lax.broadcasted_iota(jnp.int32, (rows, wide), 1)
            pairs = jnp.where((col >> 1) == row, 0.5, 0.0).astype(BF16)
            lower = contract(pairs, lower, 1, 0).astype(BF16)
            level_ref[which] = lower

    pl.semaphore_wait(barrier, greeted)
    for group in range(GROUPS):
        for number, slot in enumerate(slots):

            @pl.when(target(slot)[1])
            def _(group=group, number=number):
                kv_copy(group, number).start()

        for step in range(1, heads_axis):
            cot_copy(group, step).start()

    load_q.wait()
    load_c.wait()
    for group in range(GROUPS):
        for step in range(1, heads_axis):
            cot_copy(group, step).wait_recv()
        for number, slot in enumerate(slots):

            @pl.when(target(slot)[1])
            def _(group=group, number=number):
                other = mirror(slots, slots[number])
                kv_copy(group, other).wait_recv()

        def head_pass(head_number, carry, group=group):
            cols = pl.ds(pl.multiple_of(group * span + head_number * HEAD_DIM, HEAD_DIM), HEAD_DIM)
            query, key, value, grad = q_s[:, cols], keyset[0, :, cols], keyset[1, :, cols], cot[:, cols]
            scores = contract(key, query, 1, 1) * score_scale + bias[...]
            raised = jnp.exp(scores - jnp.max(scores, axis=0, keepdims=True))
            weights = raised * (1.0 / jnp.sum(raised, axis=0, keepdims=True))
            weights_low = weights.astype(BF16)
            att_s[:, cols] = contract(weights_low, value, 0, 0).astype(BF16)
            weight_grad = contract(value, grad, 1, 1)
            row_term = jnp.sum(weights * weight_grad, axis=0, keepdims=True)
            score_grad = (weights * (weight_grad - row_term) * score_scale).astype(BF16)
            qg_out[:, cols] = contract(score_grad, key, 0, 0).astype(BF16)
            for which, (left, right) in enumerate(((score_grad, query), (weights_low, grad))):
                set_grad = contract(left, right, 1, 0)
                own[which, :, cols] = set_grad[:block_rows]
                gsend[which, :, cols] = set_grad[block_rows:].astype(BF16)
            return carry

        lax.fori_loop(0, span // HEAD_DIM, head_pass, 0, unroll=2)
        for number, slot in enumerate(slots):

            @pl.when(target(slot)[1])
            def _(group=group, number=number):
                grad_copy(group, number).start()

        for step in range(1, heads_axis):
            att_copy(group, step).start()
        att_own(group).start()

    for group in range(GROUPS):
        for number, slot in enumerate(slots):

            @pl.when(target(slot)[1])
            def _(group=group, number=number):
                other = mirror(slots, slots[number])
                grad_copy(group, other).wait_recv()

        for which, out in enumerate((kg_out, vg_out)):
            total = own[which, :, columns(group)]
            for level in range(1, LEVELS + 1):
                spans = [slot for slot in slots if slot[0] == level]
                if not spans:
                    continue
                first, rows = spans[0][3], spans[0][4]
                count = rows * len(spans)
                row = lax.broadcasted_iota(jnp.int32, (block_rows, count), 0)
                col = lax.broadcasted_iota(jnp.int32, (block_rows, count), 1)
                spread = jnp.where(
                    (row >> level) == (col & (rows - 1)), 0.5**level, 0.0
                ).astype(BF16)
                total = total + contract(
                    spread, grecv[which, pl.ds(first, count), columns(group)], 1, 0
                )
            out[:, columns(group)] = total.astype(BF16)

    for group in range(GROUPS):
        att_own(group).wait()
        for step in range(1, heads_axis):
            cot_copy(group, step).wait_send()
            att_copy(group, step).wait()
        for number, slot in enumerate(slots):

            @pl.when(target(slot)[1])
            def _(group=group, number=number):
                kv_copy(group, number).wait_send()
                grad_copy(group, number).wait_send()


def write_out(*refs):
    copies = [
        pltpu.make_async_copy(refs[number], refs[4 + number], refs[8].at[number])
        for number in range(4)
    ]
    for copy in copies:
        copy.start()
    for copy in copies:
        copy.wait()


def local(blocks, heads_axis, queries, key_states, value_states, cotangent):
    block_rows, width = queries.shape
    slots, far_rows = span_slots(blocks, block_rows)
    levels = sorted({slot[0] for slot in slots})
    count = len(slots)
    steps = heads_axis - 1
    dma = pltpu.SemaphoreType.DMA
    anywhere = pl.BlockSpec(memory_space=pl.ANY)
    vmem = pl.BlockSpec(memory_space=pltpu.VMEM)
    scratch = [
        pltpu.VMEM((2, block_rows + far_rows, width), BF16),
        pltpu.VMEM((block_rows, width), BF16),
        pltpu.VMEM((block_rows, width), BF16),
        pltpu.VMEM((block_rows + far_rows, block_rows), F32),
        pltpu.VMEM((2, block_rows, width), F32),
        pltpu.VMEM((2, far_rows, width), BF16),
        pltpu.VMEM((2, far_rows, width), BF16),
        pltpu.VMEM((block_rows, width), BF16),
        [pltpu.VMEM((2, max(16, block_rows >> level), width), BF16) for level in levels],
        dma((3,)),
        dma,
        dma((GROUPS,)),
        dma((GROUPS, count)),
        dma((GROUPS, count)),
        dma((GROUPS, count)),
        dma((GROUPS, count)),
        dma((GROUPS, steps)),
        dma((GROUPS, steps)),
        dma((GROUPS, steps)),
        dma((GROUPS, steps)),
    ]
    part = jax.ShapeDtypeStruct(queries.shape, BF16)
    set_rows = block_rows + far_rows
    results = pl.pallas_call(
        functools.partial(kernel, blocks, heads_axis, slots, far_rows),
        out_shape=(jax.ShapeDtypeStruct(cotangent.shape, BF16), part, part, part),
        in_specs=[anywhere] * 4,
        out_specs=(anywhere, vmem, vmem, vmem),
        scratch_shapes=scratch,
        cost_estimate=pl.CostEstimate(
            flops=12 * block_rows * set_rows * width,
            bytes_accessed=16 * block_rows * width,
            transcendentals=block_rows * set_rows * width // HEAD_DIM,
        ),
        compiler_params=pltpu.CompilerParams(
            collective_id=0, has_side_effects=True, vmem_limit_bytes=60 * 2**20
        ),
    )(queries, key_states, value_states, cotangent)
    return pl.pallas_call(
        write_out,
        out_shape=tuple(jax.ShapeDtypeStruct(part.shape, part.dtype) for part in results),
        in_specs=[anywhere] * 4,
        out_specs=(anywhere,) * 4,
        scratch_shapes=[dma((4,))],
        compiler_params=pltpu.CompilerParams(vmem_limit_bytes=60 * 2**20),
    )(*results)


def solution(mesh):
    placed = (P("seq", "head"), P("seq", "head"), P("seq", "head"), P(("seq", "head"), None))
    return jax.shard_map(
        functools.partial(local, mesh.shape["seq"], mesh.shape["head"]),
        mesh=mesh,
        in_specs=placed,
        out_specs=(P(("seq", "head"), None), P("seq", "head"), P("seq", "head"), P("seq", "head")),
        check_vma=False,
    )
```

```python
import functools
import math

import jax
import jax.numpy as jnp
from jax import lax
from jax.experimental import pallas as pl
from jax.experimental.pallas import tpu as pltpu
from jax.sharding import PartitionSpec as P

HEAD_DIM = 128
LEVELS = 4
GROUPS = 2

LOG_TWO = math.log(2.0)
MASKED = -1e30
MESH = pl.DeviceIdType.MESH
F32 = jnp.float32
BF16 = jnp.bfloat16


def span_slots(blocks, block_rows):
    slots = []
    start = 0
    for level in range(1, LEVELS + 1):
        rows = max(16, block_rows >> level)
        distances = [d for d in range(2 ** (level - 1), 2**level) if d < blocks]
        for facing in (-1, 1):
            for distance in distances:
                slots.append((level, facing, distance, start, rows))
                start += rows
    return slots, start


def mirror(slots, slot):
    level, facing, distance = slot[:3]
    for number, other in enumerate(slots):
        if other[:3] == (level, -facing, distance):
            return number
    return None


def contract(left, right, left_dim, right_dim):
    return lax.dot_general(
        left, right, (((left_dim,), (right_dim,)), ((), ())), preferred_element_type=F32
    )


def kernel(
    blocks, heads_axis, slots, far_rows,
    q_hbm, k_hbm, v_hbm, c_hbm,
    att_out, qg_out, kg_out, vg_out,
    keyset, q_s, cot, bias, own, gsend, grecv, att_s, pyramid,
    in_sem, cot_own_sem, att_own_sem, ksend, krecv, gsem, gland, csend, crecv, asend, arecv,
):
    block_rows, width = q_s.shape
    out_rows = c_hbm.shape[0]
    span = width // GROUPS
    me = lax.axis_index("seq")
    my_head = lax.axis_index("head")
    score_scale = 1.0 / math.sqrt(HEAD_DIM)

    def target(slot):
        other = me + slot[1] * slot[2]
        return other, (other >= 0) & (other < blocks)

    def partner(step):
        return lax.rem(my_head + step, heads_axis)

    def columns(group):
        return pl.ds(group * span, span)

    def kv_copy(group, number):
        slot = slots[number]
        other = mirror(slots, slot)
        return pltpu.make_async_remote_copy(
            src_ref=pyramid[slot[0] - 1].at[:, :, columns(group)],
            dst_ref=keyset.at[:, pl.ds(block_rows + slots[other][3], slot[4]), columns(group)],
            send_sem=ksend.at[group, number],
            recv_sem=krecv.at[group, other],
            device_id={"seq": target(slot)[0]},
            device_id_type=MESH,
        )

    def grad_copy(group, number):
        slot = slots[number]
        other = mirror(slots, slot)
        return pltpu.make_async_remote_copy(
            src_ref=gsend.at[:, pl.ds(slot[3], slot[4]), columns(group)],
            dst_ref=grecv.at[:, pl.ds(slots[other][3], slot[4]), columns(group)],
            send_sem=gsem.at[group, number],
            recv_sem=gland.at[group, other],
            device_id={"seq": target(slot)[0]},
            device_id_type=MESH,
        )

    def cot_copy(group, step):
        other = partner(step)
        return pltpu.make_async_remote_copy(
            src_ref=c_hbm.at[:, pl.ds(pl.multiple_of(other * width + group * span, 128), span)],
            dst_ref=cot.at[pl.ds(pl.multiple_of(my_head * out_rows, 16), out_rows), columns(group)],
            send_sem=csend.at[group, step - 1],
            recv_sem=crecv.at[group, step - 1],
            device_id={"head": other},
            device_id_type=MESH,
        )

    def att_copy(group, step):
        other = partner(step)
        return pltpu.make_async_remote_copy(
            src_ref=att_s.at[pl.ds(pl.multiple_of(other * out_rows, 16), out_rows), columns(group)],
            dst_ref=att_out.at[:, pl.ds(pl.multiple_of(my_head * width + group * span, 128), span)],
            send_sem=asend.at[group, step - 1],
            recv_sem=arecv.at[group, step - 1],
            device_id={"head": other},
            device_id_type=MESH,
        )

    def att_own(group):
        return pltpu.make_async_copy(
            att_s.at[pl.ds(pl.multiple_of(my_head * out_rows, 16), out_rows), columns(group)],
            att_out.at[:, pl.ds(pl.multiple_of(my_head * width + group * span, 128), span)],
            att_own_sem.at[group],
        )

    barrier = pltpu.get_barrier_semaphore()
    greeted = heads_axis - 1
    for slot in slots:
        other, valid = target(slot)
        greeted = greeted + valid.astype(jnp.int32)

        @pl.when(valid)
        def _(other=other):
            pl.semaphore_signal(barrier, inc=1, device_id={"seq": other}, device_id_type=MESH)

    for step in range(1, heads_axis):
        pl.semaphore_signal(
            barrier, inc=1, device_id={"head": partner(step)}, device_id_type=MESH
        )

    own_rows = pl.ds(0, block_rows)
    load_k = pltpu.make_async_copy(k_hbm, keyset.at[0, own_rows], in_sem.at[0])
    load_v = pltpu.make_async_copy(v_hbm, keyset.at[1, own_rows], in_sem.at[1])
    load_q = pltpu.make_async_copy(q_hbm, q_s, in_sem.at[2])
    load_c = pltpu.make_async_copy(
        c_hbm.at[:, pl.ds(pl.multiple_of(my_head * width, 128), width)],
        cot.at[pl.ds(pl.multiple_of(my_head * out_rows, 16), out_rows)],
        cot_own_sem,
    )
    load_k.start()
    load_v.start()
    load_q.start()
    load_c.start()

    for slot in slots:
        level, _, _, first, rows = slot
        other, valid = target(slot)
        row = lax.broadcasted_iota(jnp.int32, (rows, block_rows), 0)
        shown = jnp.where(valid, level * LOG_TWO, MASKED).astype(F32)
        bias[pl.ds(block_rows + first, rows), :] = jnp.where(
            row < (block_rows >> level), shown, MASKED
        )

        @pl.when(jnp.logical_not(valid))
        def _(first=first, rows=rows):
            keyset[:, pl.ds(block_rows + first, rows), :] = jnp.zeros((2, rows, width), BF16)
            grecv[:, pl.ds(first, rows), :] = jnp.zeros((2, rows, width), BF16)

    bias[own_rows, :] = jnp.zeros((block_rows, block_rows), F32)

    load_k.wait()
    load_v.wait()
    for which in range(2):
        lower = keyset[which, own_rows, :]
        for level_ref in pyramid:
            rows, wide = level_ref.shape[1], lower.shape[0]
            row = lax.broadcasted_iota(jnp.int32, (rows, wide), 0)
            col = lax.broadcasted_iota(jnp.int32, (rows, wide), 1)
            pairs = jnp.where((col >> 1) == row, 0.5, 0.0).astype(BF16)
            lower = contract(pairs, lower, 1, 0).astype(BF16)
            level_ref[which] = lower

    pl.semaphore_wait(barrier, greeted)
    for group in range(GROUPS):
        for number, slot in enumerate(slots):

            @pl.when(target(slot)[1])
            def _(group=group, number=number):
                kv_copy(group, number).start()

        for step in range(1, heads_axis):
            cot_copy(group, step).start()

    load_q.wait()
    load_c.wait()
    for group in range(GROUPS):
        for step in range(1, heads_axis):
            cot_copy(group, step).wait_recv()
        for number, slot in enumerate(slots):

            @pl.when(target(slot)[1])
            def _(group=group, number=number):
                other = mirror(slots, slots[number])
                kv_copy(group, other).wait_recv()

        def head_pass(head_number, carry, group=group):
            cols = pl.ds(pl.multiple_of(group * span + head_number * HEAD_DIM, HEAD_DIM), HEAD_DIM)
            query, key, value, grad = q_s[:, cols], keyset[0, :, cols], keyset[1, :, cols], cot[:, cols]
            scores = contract(key, query, 1, 1) * score_scale + bias[...]
            raised = jnp.exp(scores - jnp.max(scores, axis=0, keepdims=True))
            weights = raised * (1.0 / jnp.sum(raised, axis=0, keepdims=True))
            weights_low = weights.astype(BF16)
            att_s[:, cols] = contract(weights_low, value, 0, 0).astype(BF16)
            weight_grad = contract(value, grad, 1, 1)
            row_term = jnp.sum(weights * weight_grad, axis=0, keepdims=True)
            score_grad = (weights * (weight_grad - row_term) * score_scale).astype(BF16)
            qg_out[:, cols] = contract(score_grad, key, 0, 0).astype(BF16)
            for which, (left, right) in enumerate(((score_grad, query), (weights_low, grad))):
                set_grad = contract(left, right, 1, 0)
                own[which, :, cols] = set_grad[:block_rows]
                gsend[which, :, cols] = set_grad[block_rows:].astype(BF16)
            return carry

        lax.fori_loop(0, span // HEAD_DIM, head_pass, 0, unroll=2)
        for number, slot in enumerate(slots):

            @pl.when(target(slot)[1])
            def _(group=group, number=number):
                grad_copy(group, number).start()

        for step in range(1, heads_axis):
            att_copy(group, step).start()
        att_own(group).start()

    for group in range(GROUPS):
        for number, slot in enumerate(slots):

            @pl.when(target(slot)[1])
            def _(group=group, number=number):
                other = mirror(slots, slots[number])
                grad_copy(group, other).wait_recv()

        for which, out in enumerate((kg_out, vg_out)):
            total = own[which, :, columns(group)]
            for level in range(1, LEVELS + 1):
                spans = [slot for slot in slots if slot[0] == level]
                if not spans:
                    continue
                first, rows = spans[0][3], spans[0][4]
                count = rows * len(spans)
                row = lax.broadcasted_iota(jnp.int32, (block_rows, count), 0)
                col = lax.broadcasted_iota(jnp.int32, (block_rows, count), 1)
                spread = jnp.where(
                    (row >> level) == (col & (rows - 1)), 0.5**level, 0.0
                ).astype(BF16)
                total = total + contract(
                    spread, grecv[which, pl.ds(first, count), columns(group)], 1, 0
                )
            out[:, columns(group)] = total.astype(BF16)

    for group in range(GROUPS):
        att_own(group).wait()
        for step in range(1, heads_axis):
            cot_copy(group, step).wait_send()
            att_copy(group, step).wait()
        for number, slot in enumerate(slots):

            @pl.when(target(slot)[1])
            def _(group=group, number=number):
                kv_copy(group, number).wait_send()
                grad_copy(group, number).wait_send()


def write_out(*refs):
    loads, stores = [], []
    for number in range(4):
        held = refs[8 + number]
        loads.append(pltpu.make_async_copy(refs[number], held, refs[12].at[number]))
        stores.append(pltpu.make_async_copy(held, refs[4 + number], refs[13].at[number]))
    for load in loads:
        load.start()
    for load, store in zip(loads, stores):
        load.wait()
        store.start()
    for store in stores:
        store.wait()


def local(blocks, heads_axis, queries, key_states, value_states, cotangent):
    block_rows, width = queries.shape
    slots, far_rows = span_slots(blocks, block_rows)
    levels = sorted({slot[0] for slot in slots})
    count = len(slots)
    steps = heads_axis - 1
    dma = pltpu.SemaphoreType.DMA
    anywhere = pl.BlockSpec(memory_space=pl.ANY)
    vmem = pl.BlockSpec(memory_space=pltpu.VMEM)
    scratch = [
        pltpu.VMEM((2, block_rows + far_rows, width), BF16),
        pltpu.VMEM((block_rows, width), BF16),
        pltpu.VMEM((block_rows, width), BF16),
        pltpu.VMEM((block_rows + far_rows, block_rows), F32),
        pltpu.VMEM((2, block_rows, width), F32),
        pltpu.VMEM((2, far_rows, width), BF16),
        pltpu.VMEM((2, far_rows, width), BF16),
        pltpu.VMEM((block_rows, width), BF16),
        [pltpu.VMEM((2, max(16, block_rows >> level), width), BF16) for level in levels],
        dma((3,)),
        dma,
        dma((GROUPS,)),
        dma((GROUPS, count)),
        dma((GROUPS, count)),
        dma((GROUPS, count)),
        dma((GROUPS, count)),
        dma((GROUPS, steps)),
        dma((GROUPS, steps)),
        dma((GROUPS, steps)),
        dma((GROUPS, steps)),
    ]
    part = jax.ShapeDtypeStruct(queries.shape, BF16)
    set_rows = block_rows + far_rows
    results = pl.pallas_call(
        functools.partial(kernel, blocks, heads_axis, slots, far_rows),
        out_shape=(jax.ShapeDtypeStruct(cotangent.shape, BF16), part, part, part),
        in_specs=[anywhere] * 4,
        out_specs=(anywhere, vmem, vmem, vmem),
        scratch_shapes=scratch,
        cost_estimate=pl.CostEstimate(
            flops=12 * block_rows * set_rows * width,
            bytes_accessed=16 * block_rows * width,
            transcendentals=block_rows * set_rows * width // HEAD_DIM,
        ),
        compiler_params=pltpu.CompilerParams(
            collective_id=0, has_side_effects=True, vmem_limit_bytes=60 * 2**20
        ),
    )(queries, key_states, value_states, cotangent)
    return pl.pallas_call(
        write_out,
        out_shape=tuple(jax.ShapeDtypeStruct(part.shape, part.dtype) for part in results),
        in_specs=[anywhere] * 4,
        out_specs=(anywhere,) * 4,
        scratch_shapes=[pltpu.VMEM(part.shape, BF16) for part in results] + [dma((4,)), dma((4,))],
        compiler_params=pltpu.CompilerParams(vmem_limit_bytes=60 * 2**20),
    )(*results)


def solution(mesh):
    placed = (P("seq", "head"), P("seq", "head"), P("seq", "head"), P(("seq", "head"), None))
    return jax.shard_map(
        functools.partial(local, mesh.shape["seq"], mesh.shape["head"]),
        mesh=mesh,
        in_specs=placed,
        out_specs=(P(("seq", "head"), None), P("seq", "head"), P("seq", "head"), P("seq", "head")),
        check_vma=False,
    )
```

```python
import functools
import math

import jax
import jax.numpy as jnp
from jax import lax
from jax.experimental import pallas as pl
from jax.experimental.pallas import tpu as pltpu
from jax.sharding import PartitionSpec as P

HEAD_DIM = 128
LEVELS = 4
GROUPS = 2

LOG_TWO = math.log(2.0)
MASKED = -1e30
MESH = pl.DeviceIdType.MESH
F32 = jnp.float32
BF16 = jnp.bfloat16


def rows_of(level, block_rows):
    return max(16, block_rows >> level)


class Plan:
    def __init__(self, blocks, block_rows):
        self.pairs = blocks // 2
        farthest = 2**LEVELS - 1
        self.reach = min((farthest + 1) // 2, self.pairs - 1)
        self.entries = []
        self.first = []
        self.uses = [[], []]
        self.far_rows = [0, 0]
        self.returns = [[], []]
        self.return_rows = [0, 0]
        self.entry_rows = 0
        for t in range(2):
            self.use(t, None, 1, block_rows)
        for distance in range(1, self.reach + 1):
            for offset in (distance, -distance):
                for part in range(2):
                    gaps = [abs(2 * offset + part - t) for t in range(2)]
                    levels = [gap.bit_length() if gap <= farthest else None for gap in gaps]
                    known = [level for level in levels if level is not None]
                    if not known:
                        continue
                    level = min(known)
                    rows = rows_of(level, block_rows)
                    number = len(self.entries)
                    self.entries.append((offset, part, level, rows))
                    self.first.append(self.entry_rows)
                    self.entry_rows += rows
                    self.returns[part].append((number, self.return_rows[part]))
                    self.return_rows[part] += rows
                    for t in range(2):
                        if levels[t] is not None:
                            self.use(t, number, levels[t], block_rows)

    def use(self, t, number, level, block_rows):
        rows = rows_of(level, block_rows)
        self.uses[t].append((number, level, self.far_rows[t], rows))
        self.far_rows[t] += rows

    def return_first(self, number):
        part = self.entries[number][1]
        return dict(self.returns[part])[number]


def contract(left, right, left_dim, right_dim):
    return lax.dot_general(
        left, right, (((left_dim,), (right_dim,)), ((), ())), preferred_element_type=F32
    )


def pair_matrix(rows, wide):
    row = lax.broadcasted_iota(jnp.int32, (rows, wide), 0)
    col = lax.broadcasted_iota(jnp.int32, (rows, wide), 1)
    return jnp.where((col >> 1) == row, 0.5, 0.0).astype(BF16)


def kernel(
    plan, heads_axis,
    q_hbm, k_hbm, v_hbm, c_hbm,
    att_out, qg_out, kg_out, vg_out,
    keyset, q_s, cot, bias, own, far_grad, rbuf, gsend, grecv, spread, att_s, qg_s, total_s, pyramid,
    own_sem, cot_own_sem, out_own_sem, att_own_sem, send_in, recv_in, ksend, krecv,
    gsem, gland, csend, crecv, asend, arecv, send_out, recv_out,
):
    block_rows, width = q_hbm.shape
    out_rows = c_hbm.shape[0]
    half = width // 2
    span = half // GROUPS
    entries = plan.entries
    position = lax.axis_index("seq")
    my_head = lax.axis_index("head")
    pair, mine = position // 2, position % 2
    mate = 2 * pair + 1 - mine
    crew = 2 * heads_axis
    my_seat = mine * heads_axis + my_head
    own_rows = pl.ds(0, block_rows)
    score_scale = 1.0 / math.sqrt(HEAD_DIM)

    def inside(other):
        return (other >= 0) & (other < plan.pairs)

    def rail(other):
        return {"seq": 2 * other + mine, "head": my_head}

    def seat(step):
        other = (my_seat + step) % crew
        return other // heads_axis, other % heads_axis

    def columns(group):
        return pl.ds(group * span, span)

    def side(part, group):
        return pl.ds(pl.multiple_of(part * half + group * span, 128), span)

    def remote(src, dst, send_sem, recv_sem, device):
        return pltpu.make_async_remote_copy(
            src_ref=src, dst_ref=dst, send_sem=send_sem, recv_sem=recv_sem,
            device_id=device, device_id_type=MESH,
        )

    def block_place(which, part, group):
        if which == 2:
            return q_s.at[part, :, columns(group)]
        return keyset.at[part, which, own_rows, columns(group)]

    def own_copy(which, group):
        return pltpu.make_async_copy(
            (k_hbm, v_hbm, q_hbm)[which].at[:, side(mine, group)],
            block_place(which, mine, group),
            own_sem.at[which, group],
        )

    def mate_copy(which, group):
        return remote(
            (k_hbm, v_hbm, q_hbm)[which].at[:, side(1 - mine, group)],
            block_place(which, mine, group),
            send_in.at[which, group],
            recv_in.at[which, group],
            {"seq": mate, "head": my_head},
        )

    def cot_source(part, other_head, group):
        first = other_head * width + part * half + group * span
        return c_hbm.at[:, pl.ds(pl.multiple_of(first, 128), span)]

    def cot_place(group):
        return cot.at[mine, pl.ds(pl.multiple_of(my_head * out_rows, 16), out_rows), columns(group)]

    def cot_copy(group, step):
        part, other = seat(step)
        return remote(
            cot_source(part, other, group), cot_place(group),
            csend.at[group, step - 1], crecv.at[group, step - 1],
            {"seq": 2 * pair + part, "head": other},
        )

    def cot_own(group):
        return pltpu.make_async_copy(
            cot_source(mine, my_head, group), cot_place(group), cot_own_sem.at[group]
        )

    def att_source(part, other_head, group):
        return att_s.at[
            part, pl.ds(pl.multiple_of(other_head * out_rows, 16), out_rows), columns(group)
        ]

    def att_place(group):
        first = my_head * width + mine * half + group * span
        return att_out.at[:, pl.ds(pl.multiple_of(first, 128), span)]

    def att_copy(group, step):
        part, other = seat(step)
        return remote(
            att_source(part, other, group), att_place(group),
            asend.at[group, step - 1], arecv.at[group, step - 1],
            {"seq": 2 * pair + part, "head": other},
        )

    def att_own(group):
        return pltpu.make_async_copy(
            att_source(mine, my_head, group), att_place(group), att_own_sem.at[group]
        )

    def kv_copy(group, number):
        offset, part, level, rows = entries[number]
        return remote(
            pyramid[level - 1].at[part, :, :, columns(group)],
            rbuf.at[:, pl.ds(plan.first[number], rows), columns(group)],
            ksend.at[group, number], krecv.at[group, number], rail(pair - offset),
        )

    def grad_copy(group, number):
        offset, part, level, rows = entries[number]
        return remote(
            gsend.at[:, pl.ds(plan.first[number], rows), columns(group)],
            grecv.at[part, :, pl.ds(plan.return_first(number), rows), columns(group)],
            gsem.at[group, number], gland.at[group, number], rail(pair + offset),
        )

    def result(which, part, group):
        if which == 0:
            return qg_s.at[part, :, columns(group)]
        return total_s.at[part, which - 1, :, columns(group)]

    def result_own(which, group):
        return pltpu.make_async_copy(
            result(which, mine, group),
            (qg_out, kg_out, vg_out)[which].at[:, side(mine, group)],
            out_own_sem.at[which, group],
        )

    def result_copy(which, group):
        return remote(
            result(which, 1 - mine, group),
            (qg_out, kg_out, vg_out)[which].at[:, side(mine, group)],
            send_out.at[which, group], recv_out.at[which, group],
            {"seq": mate, "head": my_head},
        )

    def make_levels(part, group):
        for which in range(2):
            lower = keyset[part, which, own_rows, columns(group)]
            for level_ref in pyramid:
                pairs = pair_matrix(level_ref.shape[2], lower.shape[0])
                lower = contract(pairs, lower, 1, 0).astype(BF16)
                level_ref[part, which, :, columns(group)] = lower

    def send_levels(part, group):
        for number, entry in enumerate(entries):
            if entry[1] == part:

                @pl.when(inside(pair - entry[0]))
                def _(number=number):
                    kv_copy(group, number).start()

    barrier = pltpu.get_barrier_semaphore()
    greeted = crew - 1
    for step in range(1, crew):
        part, other = seat(step)
        pl.semaphore_signal(
            barrier, inc=1,
            device_id={"seq": 2 * pair + part, "head": other}, device_id_type=MESH,
        )
    for distance in range(1, plan.reach + 1):
        for offset in (distance, -distance):
            valid = inside(pair + offset)
            greeted = greeted + valid.astype(jnp.int32)

            @pl.when(valid)
            def _(offset=offset):
                pl.semaphore_signal(
                    barrier, inc=1, device_id=rail(pair + offset), device_id_type=MESH
                )

    for which in range(3):
        for group in range(GROUPS):
            own_copy(which, group).start()
    for group in range(GROUPS):
        cot_own(group).start()

    pl.semaphore_wait(barrier, greeted)
    for group in range(GROUPS):
        for which in range(2):
            mate_copy(which, group).start()

    for group in range(GROUPS):
        for which in range(2):
            own_copy(which, group).wait()
        for part in range(2):

            @pl.when(mine == part)
            def _(part=part, group=group):
                make_levels(part, group)
                send_levels(part, group)

    for group in range(GROUPS):
        for which in range(2):
            mate_copy(which, group).wait_recv()
        for part in range(2):

            @pl.when(mine != part)
            def _(part=part, group=group):
                make_levels(part, group)
                send_levels(part, group)

        mate_copy(2, group).start()
        for step in range(1, crew):
            cot_copy(group, step).start()

    for t in range(2):
        bias[t, own_rows, :] = jnp.zeros((block_rows, block_rows), F32)
        for number, level, first, rows in plan.uses[t]:
            row = lax.broadcasted_iota(jnp.int32, (rows, block_rows), 0)
            shown = level * LOG_TWO
            if number is not None:
                valid = inside(pair + entries[number][0])
                shown = jnp.where(valid, shown, MASKED).astype(F32)

                @pl.when(jnp.logical_not(valid))
                def _(t=t, first=first, rows=rows):
                    keyset[t, :, pl.ds(block_rows + first, rows), :] = jnp.zeros(
                        (2, rows, half), BF16
                    )

            bias[t, pl.ds(block_rows + first, rows), :] = jnp.where(
                row < (block_rows >> level), shown, MASKED
            )
        for number, first in plan.returns[t]:
            offset, _, level, rows = entries[number]
            row = lax.broadcasted_iota(jnp.int32, (rows, block_rows), 0)
            col = lax.broadcasted_iota(jnp.int32, (rows, block_rows), 1)
            spread[t, pl.ds(first, rows), :] = jnp.where(
                (col >> level) == row, 0.5**level, 0.0
            ).astype(BF16)

            @pl.when(jnp.logical_not(inside(pair - offset)))
            def _(t=t, first=first, rows=rows):
                grecv[t, :, pl.ds(first, rows), :] = jnp.zeros((2, rows, half), BF16)

    for group in range(GROUPS):
        own_copy(2, group).wait()
        cot_own(group).wait()
        mate_copy(2, group).wait_recv()
        for step in range(1, crew):
            cot_copy(group, step).wait_recv()
        for t in range(2):
            _, _, first, rows = plan.uses[t][0]
            keyset[t, :, pl.ds(block_rows + first, rows), columns(group)] = pyramid[0][
                1 - t, :, :, columns(group)
            ]
        for number, (offset, _, level, rows) in enumerate(entries):

            @pl.when(inside(pair + offset))
            def _(group=group, number=number, level=level, rows=rows):
                kv_copy(group, number).wait_recv()
                for which in range(2):
                    fine = rbuf[which, pl.ds(plan.first[number], rows), columns(group)]
                    for t in range(2):
                        for other, use_level, first, use_rows in plan.uses[t]:
                            if other == number:
                                held = fine
                                if use_level != level:
                                    held = contract(pair_matrix(use_rows, rows), fine, 1, 0)
                                keyset[
                                    t, which, pl.ds(block_rows + first, use_rows), columns(group)
                                ] = held.astype(BF16)

        def head_pass(head_number, carry, group=group):
            cols = pl.ds(pl.multiple_of(group * span + head_number * HEAD_DIM, HEAD_DIM), HEAD_DIM)
            for t in range(2):
                set_rows = pl.ds(0, block_rows + plan.far_rows[t])
                query, grad = q_s[t, :, cols], cot[t, :, cols]
                key, value = keyset[t, 0, set_rows, cols], keyset[t, 1, set_rows, cols]
                scores = contract(key, query, 1, 1) * score_scale + bias[t, set_rows, :]
                raised = jnp.exp(scores - jnp.max(scores, axis=0, keepdims=True))
                weights = raised * (1.0 / jnp.sum(raised, axis=0, keepdims=True))
                weights_low = weights.astype(BF16)
                att_s[t, :, cols] = contract(weights_low, value, 0, 0).astype(BF16)
                weight_grad = contract(value, grad, 1, 1)
                row_term = jnp.sum(weights * weight_grad, axis=0, keepdims=True)
                score_grad = (weights * (weight_grad - row_term) * score_scale).astype(BF16)
                qg_s[t, :, cols] = contract(score_grad, key, 0, 0).astype(BF16)
                for which, (left, right) in enumerate(((score_grad, query), (weights_low, grad))):
                    set_grad = contract(left, right, 1, 0)
                    own[t, which, :, cols] = set_grad[:block_rows]
                    far_grad[t, which, pl.ds(0, plan.far_rows[t]), cols] = set_grad[
                        block_rows:
                    ].astype(BF16)
            return carry

        lax.fori_loop(0, span // HEAD_DIM, head_pass, 0)
        for number, (offset, _, level, rows) in enumerate(entries):

            @pl.when(inside(pair + offset))
            def _(group=group, number=number, level=level, rows=rows):
                for which in range(2):
                    summed = None
                    for t in range(2):
                        for other, use_level, first, use_rows in plan.uses[t]:
                            if other == number:
                                term = far_grad[t, which, pl.ds(first, use_rows), columns(group)]
                                if use_level != level:
                                    term = contract(pair_matrix(use_rows, rows), term, 0, 0)
                                term = term.astype(F32)
                                summed = term if summed is None else summed + term
                    gsend[which, pl.ds(plan.first[number], rows), columns(group)] = summed.astype(
                        BF16
                    )
                grad_copy(group, number).start()

        for step in range(1, crew):
            att_copy(group, step).start()
        att_own(group).start()
        result_copy(0, group).start()
        result_own(0, group).start()

    for group in range(GROUPS):
        for number, (offset, _, _, _) in enumerate(entries):

            @pl.when(inside(pair - offset))
            def _(group=group, number=number):
                grad_copy(group, number).wait_recv()

        for u in range(2):
            _, _, first, rows = plan.uses[1 - u][0]
            near = pair_matrix(rows, block_rows)
            returned = pl.ds(0, plan.return_rows[u])
            for which in range(2):
                total = own[u, which, :, columns(group)]
                total = total + contract(
                    near, far_grad[1 - u, which, pl.ds(first, rows), columns(group)], 0, 0
                )
                total = total + contract(
                    spread[u, returned, :], grecv[u, which, returned, columns(group)], 0, 0
                )
                total_s[u, which, :, columns(group)] = total.astype(BF16)
        for which in (1, 2):
            result_copy(which, group).start()
            result_own(which, group).start()

    for group in range(GROUPS):
        att_own(group).wait()
        for which in range(3):
            result_own(which, group).wait()
            result_copy(which, group).wait()
            mate_copy(which, group).wait_send()
        for step in range(1, crew):
            cot_copy(group, step).wait_send()
            att_copy(group, step).wait()
        for number, (offset, _, _, _) in enumerate(entries):

            @pl.when(inside(pair - offset))
            def _(group=group, number=number):
                kv_copy(group, number).wait_send()

            @pl.when(inside(pair + offset))
            def _(group=group, number=number):
                grad_copy(group, number).wait_send()


def write_out(*refs):
    loads, stores = [], []
    for number in range(4):
        held = refs[8 + number]
        loads.append(pltpu.make_async_copy(refs[number], held, refs[12].at[number]))
        stores.append(pltpu.make_async_copy(held, refs[4 + number], refs[13].at[number]))
    for load in loads:
        load.start()
    for load, store in zip(loads, stores):
        load.wait()
        store.start()
    for store in stores:
        store.wait()


def local(blocks, heads_axis, queries, key_states, value_states, cotangent):
    block_rows, width = queries.shape
    plan = Plan(blocks, block_rows)
    half = width // 2
    count = len(plan.entries)
    far_rows, return_rows = max(plan.far_rows), max(plan.return_rows)
    set_rows = block_rows + far_rows
    levels = max(entry[2] for entry in plan.entries)
    steps = 2 * heads_axis - 1
    dma = pltpu.SemaphoreType.DMA
    anywhere = pl.BlockSpec(memory_space=pl.ANY)
    scratch = [
        pltpu.VMEM((2, 2, set_rows, half), BF16),
        pltpu.VMEM((2, block_rows, half), BF16),
        pltpu.VMEM((2, block_rows, half), BF16),
        pltpu.VMEM((2, set_rows, block_rows), F32),
        pltpu.VMEM((2, 2, block_rows, half), F32),
        pltpu.VMEM((2, 2, far_rows, half), BF16),
        pltpu.VMEM((2, plan.entry_rows, half), BF16),
        pltpu.VMEM((2, plan.entry_rows, half), BF16),
        pltpu.VMEM((2, 2, return_rows, half), BF16),
        pltpu.VMEM((2, return_rows, block_rows), BF16),
        pltpu.VMEM((2, block_rows, half), BF16),
        pltpu.VMEM((2, block_rows, half), BF16),
        pltpu.VMEM((2, 2, block_rows, half), BF16),
        [
            pltpu.VMEM((2, 2, rows_of(level, block_rows), half), BF16)
            for level in range(1, levels + 1)
        ],
        dma((3, GROUPS)),
        dma((GROUPS,)),
        dma((3, GROUPS)),
        dma((GROUPS,)),
        dma((3, GROUPS)),
        dma((3, GROUPS)),
        dma((GROUPS, count)),
        dma((GROUPS, count)),
        dma((GROUPS, count)),
        dma((GROUPS, count)),
        dma((GROUPS, steps)),
        dma((GROUPS, steps)),
        dma((GROUPS, steps)),
        dma((GROUPS, steps)),
        dma((3, GROUPS)),
        dma((3, GROUPS)),
    ]
    part = jax.ShapeDtypeStruct(queries.shape, BF16)
    results = pl.pallas_call(
        functools.partial(kernel, plan, heads_axis),
        out_shape=(jax.ShapeDtypeStruct(cotangent.shape, BF16), part, part, part),
        in_specs=[anywhere] * 4,
        out_specs=(anywhere,) * 4,
        scratch_shapes=scratch,
        cost_estimate=pl.CostEstimate(
            flops=12 * block_rows * set_rows * width,
            bytes_accessed=16 * block_rows * width,
            transcendentals=block_rows * set_rows * width // HEAD_DIM,
        ),
        compiler_params=pltpu.CompilerParams(
            collective_id=0, has_side_effects=True, vmem_limit_bytes=60 * 2**20
        ),
    )(queries, key_states, value_states, cotangent)
    return pl.pallas_call(
        write_out,
        out_shape=tuple(jax.ShapeDtypeStruct(part.shape, part.dtype) for part in results),
        in_specs=[anywhere] * 4,
        out_specs=(anywhere,) * 4,
        scratch_shapes=[pltpu.VMEM(part.shape, BF16) for part in results] + [dma((4,)), dma((4,))],
        compiler_params=pltpu.CompilerParams(vmem_limit_bytes=60 * 2**20),
    )(*results)


def solution(mesh):
    placed = (P("seq", "head"), P("seq", "head"), P("seq", "head"), P(("seq", "head"), None))
    return jax.shard_map(
        functools.partial(local, mesh.shape["seq"], mesh.shape["head"]),
        mesh=mesh,
        in_specs=placed,
        out_specs=(P(("seq", "head"), None), P("seq", "head"), P("seq", "head"), P("seq", "head")),
        check_vma=False,
    )
```

```python
import functools
import math

import jax
import jax.numpy as jnp
from jax import lax
from jax.experimental import pallas as pl
from jax.experimental.pallas import tpu as pltpu
from jax.sharding import PartitionSpec as P

HEAD_DIM = 128
LEVELS = 4
GROUPS = 4

LOG_TWO = math.log(2.0)
MASKED = -1e30
MESH = pl.DeviceIdType.MESH
F32 = jnp.float32
BF16 = jnp.bfloat16


def rows_of(level, block_rows):
    return max(16, block_rows >> level)


class Plan:
    def __init__(self, blocks, block_rows):
        self.pairs = blocks // 2
        farthest = 2**LEVELS - 1
        self.reach = min((farthest + 1) // 2, self.pairs - 1)
        self.entries = []
        self.first = []
        self.uses = [[], []]
        self.far_rows = [0, 0]
        self.returns = [[], []]
        self.return_rows = [0, 0]
        self.entry_rows = 0
        for t in range(2):
            self.use(t, None, 1, block_rows)
        for distance in range(1, self.reach + 1):
            for offset in (distance, -distance):
                for part in range(2):
                    gaps = [abs(2 * offset + part - t) for t in range(2)]
                    levels = [gap.bit_length() if gap <= farthest else None for gap in gaps]
                    known = [level for level in levels if level is not None]
                    if not known:
                        continue
                    level = min(known)
                    rows = rows_of(level, block_rows)
                    number = len(self.entries)
                    self.entries.append((offset, part, level, rows))
                    self.first.append(self.entry_rows)
                    self.entry_rows += rows
                    self.returns[part].append((number, self.return_rows[part]))
                    self.return_rows[part] += rows
                    for t in range(2):
                        if levels[t] is not None:
                            self.use(t, number, levels[t], block_rows)

    def use(self, t, number, level, block_rows):
        rows = rows_of(level, block_rows)
        self.uses[t].append((number, level, self.far_rows[t], rows))
        self.far_rows[t] += rows

    def return_first(self, number):
        part = self.entries[number][1]
        return dict(self.returns[part])[number]


def contract(left, right, left_dim, right_dim):
    return lax.dot_general(
        left, right, (((left_dim,), (right_dim,)), ((), ())), preferred_element_type=F32
    )


def pair_matrix(rows, wide):
    row = lax.broadcasted_iota(jnp.int32, (rows, wide), 0)
    col = lax.broadcasted_iota(jnp.int32, (rows, wide), 1)
    return jnp.where((col >> 1) == row, 0.5, 0.0).astype(BF16)


def kernel(
    plan, heads_axis,
    q_hbm, k_hbm, v_hbm, c_hbm,
    att_out, qg_out, kg_out, vg_out,
    keyset, q_s, cot, bias, own, far_grad, rbuf, gsend, grecv, spread, att_s, qg_s, total_s, pyramid,
    own_sem, cot_own_sem, out_own_sem, att_own_sem, send_in, recv_in, ksend, krecv,
    gsem, gland, csend, crecv, asend, arecv, send_out, recv_out,
):
    block_rows, width = q_hbm.shape
    out_rows = c_hbm.shape[0]
    half = width // 2
    span = half // GROUPS
    entries = plan.entries
    position = lax.axis_index("seq")
    my_head = lax.axis_index("head")
    pair, mine = position // 2, position % 2
    mate = 2 * pair + 1 - mine
    crew = 2 * heads_axis
    my_seat = mine * heads_axis + my_head
    own_rows = pl.ds(0, block_rows)
    score_scale = 1.0 / math.sqrt(HEAD_DIM)

    def inside(other):
        return (other >= 0) & (other < plan.pairs)

    def rail(other):
        return {"seq": 2 * other + mine, "head": my_head}

    def seat(step):
        other = (my_seat + step) % crew
        return other // heads_axis, other % heads_axis

    def columns(group):
        return pl.ds(group * span, span)

    def side(part, group):
        return pl.ds(pl.multiple_of(part * half + group * span, 128), span)

    def remote(src, dst, send_sem, recv_sem, device):
        return pltpu.make_async_remote_copy(
            src_ref=src, dst_ref=dst, send_sem=send_sem, recv_sem=recv_sem,
            device_id=device, device_id_type=MESH,
        )

    def block_place(which, part, group):
        if which == 2:
            return q_s.at[part, :, columns(group)]
        return keyset.at[part, which, own_rows, columns(group)]

    def own_copy(which, group):
        return pltpu.make_async_copy(
            (k_hbm, v_hbm, q_hbm)[which].at[:, side(mine, group)],
            block_place(which, mine, group),
            own_sem.at[which, group],
        )

    def mate_copy(which, group):
        return remote(
            (k_hbm, v_hbm, q_hbm)[which].at[:, side(1 - mine, group)],
            block_place(which, mine, group),
            send_in.at[which, group],
            recv_in.at[which, group],
            {"seq": mate, "head": my_head},
        )

    def cot_source(part, other_head, group):
        first = other_head * width + part * half + group * span
        return c_hbm.at[:, pl.ds(pl.multiple_of(first, 128), span)]

    def cot_place(group):
        return cot.at[mine, pl.ds(pl.multiple_of(my_head * out_rows, 16), out_rows), columns(group)]

    def cot_copy(group, step):
        part, other = seat(step)
        return remote(
            cot_source(part, other, group), cot_place(group),
            csend.at[group, step - 1], crecv.at[group, step - 1],
            {"seq": 2 * pair + part, "head": other},
        )

    def cot_own(group):
        return pltpu.make_async_copy(
            cot_source(mine, my_head, group), cot_place(group), cot_own_sem.at[group]
        )

    def att_source(part, other_head, group):
        return att_s.at[
            part, pl.ds(pl.multiple_of(other_head * out_rows, 16), out_rows), columns(group)
        ]

    def att_place(group):
        first = my_head * width + mine * half + group * span
        return att_out.at[:, pl.ds(pl.multiple_of(first, 128), span)]

    def att_copy(group, step):
        part, other = seat(step)
        return remote(
            att_source(part, other, group), att_place(group),
            asend.at[group, step - 1], arecv.at[group, step - 1],
            {"seq": 2 * pair + part, "head": other},
        )

    def att_own(group):
        return pltpu.make_async_copy(
            att_source(mine, my_head, group), att_place(group), att_own_sem.at[group]
        )

    def kv_copy(group, number):
        offset, part, level, rows = entries[number]
        return remote(
            pyramid[level - 1].at[part, :, :, columns(group)],
            rbuf.at[:, pl.ds(plan.first[number], rows), columns(group)],
            ksend.at[group, number], krecv.at[group, number], rail(pair - offset),
        )

    def grad_copy(group, number):
        offset, part, level, rows = entries[number]
        return remote(
            gsend.at[:, pl.ds(plan.first[number], rows), columns(group)],
            grecv.at[part, :, pl.ds(plan.return_first(number), rows), columns(group)],
            gsem.at[group, number], gland.at[group, number], rail(pair + offset),
        )

    def result(which, part, group):
        if which == 0:
            return qg_s.at[part, :, columns(group)]
        return total_s.at[part, which - 1, :, columns(group)]

    def result_own(which, group):
        return pltpu.make_async_copy(
            result(which, mine, group),
            (qg_out, kg_out, vg_out)[which].at[:, side(mine, group)],
            out_own_sem.at[which, group],
        )

    def result_copy(which, group):
        return remote(
            result(which, 1 - mine, group),
            (qg_out, kg_out, vg_out)[which].at[:, side(mine, group)],
            send_out.at[which, group], recv_out.at[which, group],
            {"seq": mate, "head": my_head},
        )

    def make_levels(part, group):
        for which in range(2):
            lower = keyset[part, which, own_rows, columns(group)]
            for level_ref in pyramid:
                pairs = pair_matrix(level_ref.shape[2], lower.shape[0])
                lower = contract(pairs, lower, 1, 0).astype(BF16)
                level_ref[part, which, :, columns(group)] = lower

    def send_levels(part, group):
        for number, entry in enumerate(entries):
            if entry[1] == part:

                @pl.when(inside(pair - entry[0]))
                def _(number=number):
                    kv_copy(group, number).start()

    def finish(group):
        for number, (offset, _, _, _) in enumerate(entries):

            @pl.when(inside(pair - offset))
            def _(group=group, number=number):
                grad_copy(group, number).wait_recv()

        for u in range(2):
            _, _, first, rows = plan.uses[1 - u][0]
            near = pair_matrix(rows, block_rows)
            returned = pl.ds(0, plan.return_rows[u])
            for which in range(2):
                total = own[u, which, :, columns(group)]
                total = total + contract(
                    near, far_grad[1 - u, which, pl.ds(first, rows), columns(group)], 0, 0
                )
                total = total + contract(
                    spread[u, returned, :], grecv[u, which, returned, columns(group)], 0, 0
                )
                total_s[u, which, :, columns(group)] = total.astype(BF16)
        for which in (1, 2):
            result_copy(which, group).start()
            result_own(which, group).start()

    barrier = pltpu.get_barrier_semaphore()
    greeted = crew - 1
    for step in range(1, crew):
        part, other = seat(step)
        pl.semaphore_signal(
            barrier, inc=1,
            device_id={"seq": 2 * pair + part, "head": other}, device_id_type=MESH,
        )
    for distance in range(1, plan.reach + 1):
        for offset in (distance, -distance):
            valid = inside(pair + offset)
            greeted = greeted + valid.astype(jnp.int32)

            @pl.when(valid)
            def _(offset=offset):
                pl.semaphore_signal(
                    barrier, inc=1, device_id=rail(pair + offset), device_id_type=MESH
                )

    for which in range(3):
        for group in range(GROUPS):
            own_copy(which, group).start()
    for group in range(GROUPS):
        cot_own(group).start()

    pl.semaphore_wait(barrier, greeted)
    for group in range(GROUPS):
        for which in range(2):
            mate_copy(which, group).start()

    for group in range(GROUPS):
        for which in range(2):
            own_copy(which, group).wait()
        for part in range(2):

            @pl.when(mine == part)
            def _(part=part, group=group):
                make_levels(part, group)
                send_levels(part, group)

    for group in range(GROUPS):
        for which in range(2):
            mate_copy(which, group).wait_recv()
        for part in range(2):

            @pl.when(mine != part)
            def _(part=part, group=group):
                make_levels(part, group)
                send_levels(part, group)

        mate_copy(2, group).start()
        for step in range(1, crew):
            cot_copy(group, step).start()

    for t in range(2):
        bias[t, own_rows, :] = jnp.zeros((block_rows, block_rows), F32)
        for number, level, first, rows in plan.uses[t]:
            row = lax.broadcasted_iota(jnp.int32, (rows, block_rows), 0)
            shown = float(level)
            if number is not None:
                valid = inside(pair + entries[number][0])
                shown = jnp.where(valid, shown, MASKED).astype(F32)

                @pl.when(jnp.logical_not(valid))
                def _(t=t, first=first, rows=rows):
                    keyset[t, :, pl.ds(block_rows + first, rows), :] = jnp.zeros(
                        (2, rows, half), BF16
                    )

            bias[t, pl.ds(block_rows + first, rows), :] = jnp.where(
                row < (block_rows >> level), shown, MASKED
            )
        for number, first in plan.returns[t]:
            offset, _, level, rows = entries[number]
            row = lax.broadcasted_iota(jnp.int32, (rows, block_rows), 0)
            col = lax.broadcasted_iota(jnp.int32, (rows, block_rows), 1)
            spread[t, pl.ds(first, rows), :] = jnp.where(
                (col >> level) == row, 0.5**level, 0.0
            ).astype(BF16)

            @pl.when(jnp.logical_not(inside(pair - offset)))
            def _(t=t, first=first, rows=rows):
                grecv[t, :, pl.ds(first, rows), :] = jnp.zeros((2, rows, half), BF16)

    for group in range(GROUPS):
        own_copy(2, group).wait()
        cot_own(group).wait()
        mate_copy(2, group).wait_recv()
        for step in range(1, crew):
            cot_copy(group, step).wait_recv()
        for t in range(2):
            _, _, first, rows = plan.uses[t][0]
            keyset[t, :, pl.ds(block_rows + first, rows), columns(group)] = pyramid[0][
                1 - t, :, :, columns(group)
            ]
        for number, (offset, _, level, rows) in enumerate(entries):

            @pl.when(inside(pair + offset))
            def _(group=group, number=number, level=level, rows=rows):
                kv_copy(group, number).wait_recv()
                for which in range(2):
                    fine = rbuf[which, pl.ds(plan.first[number], rows), columns(group)]
                    for t in range(2):
                        for other, use_level, first, use_rows in plan.uses[t]:
                            if other == number:
                                held = fine
                                if use_level != level:
                                    held = contract(pair_matrix(use_rows, rows), fine, 1, 0)
                                keyset[
                                    t, which, pl.ds(block_rows + first, use_rows), columns(group)
                                ] = held.astype(BF16)

        def head_pass(head_number, carry, group=group):
            cols = pl.ds(pl.multiple_of(group * span + head_number * HEAD_DIM, HEAD_DIM), HEAD_DIM)
            both = range(2)
            set_rows = [pl.ds(0, block_rows + plan.far_rows[t]) for t in both]
            query, grad = [q_s[t, :, cols] for t in both], [cot[t, :, cols] for t in both]
            key = [keyset[t, 0, set_rows[t], cols] for t in both]
            value = [keyset[t, 1, set_rows[t], cols] for t in both]
            scores = [
                contract(key[t], query[t], 1, 1) * (score_scale / LOG_TWO) + bias[t, set_rows[t], :]
                for t in both
            ]
            weight_grad = [contract(value[t], grad[t], 1, 1) for t in both]
            raised = [jnp.exp2(part - jnp.max(part, axis=0, keepdims=True)) for part in scores]
            weights = [part * (1.0 / jnp.sum(part, axis=0, keepdims=True)) for part in raised]
            weights_low = [part.astype(BF16) for part in weights]
            row_term = [
                jnp.sum(weights[t] * weight_grad[t], axis=0, keepdims=True) for t in both
            ]
            score_grad = [
                (weights[t] * ((weight_grad[t] - row_term[t]) * score_scale)).astype(BF16)
                for t in both
            ]
            for t in both:
                att_s[t, :, cols] = contract(weights_low[t], value[t], 0, 0).astype(BF16)
                qg_s[t, :, cols] = contract(score_grad[t], key[t], 0, 0).astype(BF16)
                for which, (left, right) in enumerate(
                    ((score_grad[t], query[t]), (weights_low[t], grad[t]))
                ):
                    set_grad = contract(left, right, 1, 0)
                    own[t, which, :, cols] = set_grad[:block_rows]
                    far_grad[t, which, pl.ds(0, plan.far_rows[t]), cols] = set_grad[
                        block_rows:
                    ].astype(BF16)
            return carry

        lax.fori_loop(0, span // HEAD_DIM, head_pass, 0)
        for number, (offset, _, level, rows) in enumerate(entries):

            @pl.when(inside(pair + offset))
            def _(group=group, number=number, level=level, rows=rows):
                for which in range(2):
                    summed = None
                    for t in range(2):
                        for other, use_level, first, use_rows in plan.uses[t]:
                            if other == number:
                                term = far_grad[t, which, pl.ds(first, use_rows), columns(group)]
                                if use_level != level:
                                    term = contract(pair_matrix(use_rows, rows), term, 0, 0)
                                term = term.astype(F32)
                                summed = term if summed is None else summed + term
                    gsend[which, pl.ds(plan.first[number], rows), columns(group)] = summed.astype(
                        BF16
                    )
                grad_copy(group, number).start()

        for step in range(1, crew):
            att_copy(group, step).start()
        att_own(group).start()
        result_copy(0, group).start()
        result_own(0, group).start()
        if group >= 2:
            finish(group - 2)

    for group in range(max(0, GROUPS - 2), GROUPS):
        finish(group)

    for group in range(GROUPS):
        att_own(group).wait()
        for which in range(3):
            result_own(which, group).wait()
            result_copy(which, group).wait()
            mate_copy(which, group).wait_send()
        for step in range(1, crew):
            cot_copy(group, step).wait_send()
            att_copy(group, step).wait()
        for number, (offset, _, _, _) in enumerate(entries):

            @pl.when(inside(pair - offset))
            def _(group=group, number=number):
                kv_copy(group, number).wait_send()

            @pl.when(inside(pair + offset))
            def _(group=group, number=number):
                grad_copy(group, number).wait_send()


def write_out(*refs):
    loads, stores = [], []
    for number in range(4):
        held = refs[8 + number]
        loads.append(pltpu.make_async_copy(refs[number], held, refs[12].at[number]))
        stores.append(pltpu.make_async_copy(held, refs[4 + number], refs[13].at[number]))
    for load in loads:
        load.start()
    for load, store in zip(loads, stores):
        load.wait()
        store.start()
    for store in stores:
        store.wait()


def local(blocks, heads_axis, queries, key_states, value_states, cotangent):
    block_rows, width = queries.shape
    plan = Plan(blocks, block_rows)
    half = width // 2
    count = len(plan.entries)
    far_rows, return_rows = max(plan.far_rows), max(plan.return_rows)
    set_rows = block_rows + far_rows
    levels = max(entry[2] for entry in plan.entries)
    steps = 2 * heads_axis - 1
    dma = pltpu.SemaphoreType.DMA
    anywhere = pl.BlockSpec(memory_space=pl.ANY)
    scratch = [
        pltpu.VMEM((2, 2, set_rows, half), BF16),
        pltpu.VMEM((2, block_rows, half), BF16),
        pltpu.VMEM((2, block_rows, half), BF16),
        pltpu.VMEM((2, set_rows, block_rows), F32),
        pltpu.VMEM((2, 2, block_rows, half), F32),
        pltpu.VMEM((2, 2, far_rows, half), BF16),
        pltpu.VMEM((2, plan.entry_rows, half), BF16),
        pltpu.VMEM((2, plan.entry_rows, half), BF16),
        pltpu.VMEM((2, 2, return_rows, half), BF16),
        pltpu.VMEM((2, return_rows, block_rows), BF16),
        pltpu.VMEM((2, block_rows, half), BF16),
        pltpu.VMEM((2, block_rows, half), BF16),
        pltpu.VMEM((2, 2, block_rows, half), BF16),
        [
            pltpu.VMEM((2, 2, rows_of(level, block_rows), half), BF16)
            for level in range(1, levels + 1)
        ],
        dma((3, GROUPS)),
        dma((GROUPS,)),
        dma((3, GROUPS)),
        dma((GROUPS,)),
        dma((3, GROUPS)),
        dma((3, GROUPS)),
        dma((GROUPS, count)),
        dma((GROUPS, count)),
        dma((GROUPS, count)),
        dma((GROUPS, count)),
        dma((GROUPS, steps)),
        dma((GROUPS, steps)),
        dma((GROUPS, steps)),
        dma((GROUPS, steps)),
        dma((3, GROUPS)),
        dma((3, GROUPS)),
    ]
    part = jax.ShapeDtypeStruct(queries.shape, BF16)
    results = pl.pallas_call(
        functools.partial(kernel, plan, heads_axis),
        out_shape=(jax.ShapeDtypeStruct(cotangent.shape, BF16), part, part, part),
        in_specs=[anywhere] * 4,
        out_specs=(anywhere,) * 4,
        scratch_shapes=scratch,
        cost_estimate=pl.CostEstimate(
            flops=12 * block_rows * set_rows * width,
            bytes_accessed=16 * block_rows * width,
            transcendentals=block_rows * set_rows * width // HEAD_DIM,
        ),
        compiler_params=pltpu.CompilerParams(
            collective_id=0, has_side_effects=True, vmem_limit_bytes=60 * 2**20
        ),
    )(queries, key_states, value_states, cotangent)
    return pl.pallas_call(
        write_out,
        out_shape=tuple(jax.ShapeDtypeStruct(part.shape, part.dtype) for part in results),
        in_specs=[anywhere] * 4,
        out_specs=(anywhere,) * 4,
        scratch_shapes=[pltpu.VMEM(part.shape, BF16) for part in results] + [dma((4,)), dma((4,))],
        compiler_params=pltpu.CompilerParams(vmem_limit_bytes=60 * 2**20),
    )(*results)


def solution(mesh):
    placed = (P("seq", "head"), P("seq", "head"), P("seq", "head"), P(("seq", "head"), None))
    return jax.shard_map(
        functools.partial(local, mesh.shape["seq"], mesh.shape["head"]),
        mesh=mesh,
        in_specs=placed,
        out_specs=(P(("seq", "head"), None), P("seq", "head"), P("seq", "head"), P("seq", "head")),
        check_vma=False,
    )
```

```python
import functools
import math

import jax
import jax.numpy as jnp
from jax import lax
from jax.experimental import pallas as pl
from jax.experimental.pallas import tpu as pltpu
from jax.sharding import PartitionSpec as P

HEAD_DIM = 128
LEVELS = 4
GROUPS = 4
CHUNK = 2

LOG_TWO = math.log(2.0)
MASKED = -1e30
MESH = pl.DeviceIdType.MESH
F32 = jnp.float32
BF16 = jnp.bfloat16


def rows_of(level, block_rows):
    return max(16, block_rows >> level)


class Plan:
    def __init__(self, blocks, block_rows):
        self.pairs = blocks // 2
        farthest = 2**LEVELS - 1
        self.reach = min((farthest + 1) // 2, self.pairs - 1)
        self.entries = []
        self.first = []
        self.uses = [[], []]
        self.far_rows = [0, 0]
        self.messages = []
        self.entry_rows = 0
        for t in range(2):
            self.use(t, None, 1, block_rows)
        for distance in range(1, self.reach + 1):
            for offset in (distance, -distance):
                start = self.entry_rows
                for part in range(2):
                    gaps = [abs(2 * offset + part - t) for t in range(2)]
                    levels = [gap.bit_length() if gap <= farthest else None for gap in gaps]
                    known = [level for level in levels if level is not None]
                    if not known:
                        continue
                    level = min(known)
                    rows = rows_of(level, block_rows)
                    number = len(self.entries)
                    self.entries.append((offset, part, level, rows))
                    self.first.append(self.entry_rows)
                    self.entry_rows += rows
                    for t in range(2):
                        if levels[t] is not None:
                            self.use(t, number, levels[t], block_rows)
                self.messages.append((offset, start, self.entry_rows - start))

    def use(self, t, number, level, block_rows):
        rows = rows_of(level, block_rows)
        self.uses[t].append((number, level, self.far_rows[t], rows))
        self.far_rows[t] += rows


def contract(left, right, left_dim, right_dim):
    return lax.dot_general(
        left, right, (((left_dim,), (right_dim,)), ((), ())), preferred_element_type=F32
    )


def pair_matrix(rows, wide):
    row = lax.broadcasted_iota(jnp.int32, (rows, wide), 0)
    col = lax.broadcasted_iota(jnp.int32, (rows, wide), 1)
    return jnp.where((col >> 1) == row, 0.5, 0.0).astype(BF16)


def kernel(
    plan, heads_axis,
    q_hbm, k_hbm, v_hbm, c_hbm,
    att_out, qg_out, kg_out, vg_out,
    keyset, q_s, cot, bias, own, far_grad, rbuf, gsend, grecv, spread, held_s, att_s, qg_s, total_s, pyramid,
    own_sem, cot_own_sem, out_own_sem, att_own_sem, send_in, recv_in, ksend, krecv,
    gsem, gland, csend, crecv, asend, arecv, send_out, recv_out,
):
    block_rows, width = q_hbm.shape
    out_rows = c_hbm.shape[0]
    half = width // 2
    span = half // GROUPS
    wide = CHUNK * span
    chunks = GROUPS // CHUNK
    entries = plan.entries
    position = lax.axis_index("seq")
    my_head = lax.axis_index("head")
    pair, mine = position // 2, position % 2
    mate = 2 * pair + 1 - mine
    crew = 2 * heads_axis
    my_seat = mine * heads_axis + my_head
    own_rows = pl.ds(0, block_rows)
    score_scale = 1.0 / math.sqrt(HEAD_DIM)

    def inside(other):
        return (other >= 0) & (other < plan.pairs)

    def rail(other):
        return {"seq": 2 * other + mine, "head": my_head}

    def seat(step):
        other = (my_seat + step) % crew
        return other // heads_axis, other % heads_axis

    def columns(group):
        return pl.ds(group * span, span)

    def side(part, group):
        return pl.ds(pl.multiple_of(part * half + group * span, 128), span)

    def remote(src, dst, send_sem, recv_sem, device):
        return pltpu.make_async_remote_copy(
            src_ref=src, dst_ref=dst, send_sem=send_sem, recv_sem=recv_sem,
            device_id=device, device_id_type=MESH,
        )

    def block_place(which, part, group):
        if which == 2:
            return q_s.at[part, :, columns(group)]
        return keyset.at[part, which, own_rows, columns(group)]

    def own_copy(which, group):
        return pltpu.make_async_copy(
            (k_hbm, v_hbm, q_hbm)[which].at[:, side(mine, group)],
            block_place(which, mine, group),
            own_sem.at[which, group],
        )

    def mate_copy(which, group):
        return remote(
            (k_hbm, v_hbm, q_hbm)[which].at[:, side(1 - mine, group)],
            block_place(which, mine, group),
            send_in.at[which, group],
            recv_in.at[which, group],
            {"seq": mate, "head": my_head},
        )

    def cot_source(part, other_head, chunk):
        first = other_head * width + part * half + chunk * wide
        return c_hbm.at[:, pl.ds(pl.multiple_of(first, 128), wide)]

    def cot_place(chunk):
        return cot.at[mine, pl.ds(pl.multiple_of(my_head * out_rows, 16), out_rows), pl.ds(chunk * wide, wide)]

    def cot_copy(chunk, step):
        part, other = seat(step)
        return remote(
            cot_source(part, other, chunk), cot_place(chunk),
            csend.at[chunk, step - 1], crecv.at[chunk, step - 1],
            {"seq": 2 * pair + part, "head": other},
        )

    def cot_own(chunk):
        return pltpu.make_async_copy(
            cot_source(mine, my_head, chunk), cot_place(chunk), cot_own_sem.at[chunk]
        )

    def att_source(part, other_head, chunk):
        return att_s.at[
            part, pl.ds(pl.multiple_of(other_head * out_rows, 16), out_rows), pl.ds(chunk * wide, wide)
        ]

    def att_place(chunk):
        first = my_head * width + mine * half + chunk * wide
        return att_out.at[:, pl.ds(pl.multiple_of(first, 128), wide)]

    def att_copy(chunk, step):
        part, other = seat(step)
        return remote(
            att_source(part, other, chunk), att_place(chunk),
            asend.at[chunk, step - 1], arecv.at[chunk, step - 1],
            {"seq": 2 * pair + part, "head": other},
        )

    def att_own(chunk):
        return pltpu.make_async_copy(
            att_source(mine, my_head, chunk), att_place(chunk), att_own_sem.at[chunk]
        )

    def kv_copy(group, number):
        offset, part, level, rows = entries[number]
        return remote(
            pyramid[level - 1].at[part, :, :, columns(group)],
            rbuf.at[:, pl.ds(plan.first[number], rows), columns(group)],
            ksend.at[group, number], krecv.at[group, number], rail(pair - offset),
        )

    def grad_copy(group, number):
        offset, first, rows = plan.messages[number]
        place = (slice(None), pl.ds(first, rows), columns(group))
        return remote(
            gsend.at[place], grecv.at[place],
            gsem.at[group, number], gland.at[group, number], rail(pair + offset),
        )

    def result(which, part, group):
        if which == 0:
            return qg_s.at[part, :, columns(group)]
        return total_s.at[part, which - 1, :, columns(group)]

    def result_own(which, group):
        return pltpu.make_async_copy(
            result(which, mine, group),
            (qg_out, kg_out, vg_out)[which].at[:, side(mine, group)],
            out_own_sem.at[which, group],
        )

    def result_copy(which, group):
        return remote(
            result(which, 1 - mine, group),
            (qg_out, kg_out, vg_out)[which].at[:, side(mine, group)],
            send_out.at[which, group], recv_out.at[which, group],
            {"seq": mate, "head": my_head},
        )

    def make_levels(part, group):
        for which in range(2):
            lower = keyset[part, which, own_rows, columns(group)]
            for level_ref in pyramid:
                pairs = pair_matrix(level_ref.shape[2], lower.shape[0])
                lower = contract(pairs, lower, 1, 0).astype(BF16)
                level_ref[part, which, :, columns(group)] = lower

    def send_levels(part, group):
        for number, entry in enumerate(entries):

            @pl.when((part == entry[1]) & inside(pair - entry[0]))
            def _(number=number):
                kv_copy(group, number).start()

    def send_near(group):
        for which in range(2):
            mate_copy(which, group).start()

    def send_own(group):
        for which in range(2):
            own_copy(which, group).wait()
        make_levels(mine, group)
        send_levels(mine, group)

    def send_rest(group):
        mate_copy(2, group).start()
        if group % CHUNK == 0:
            for step in range(1, crew):
                cot_copy(group // CHUNK, step).start()

    def send_mate(group):
        for which in range(2):
            mate_copy(which, group).wait_recv()
        make_levels(1 - mine, group)
        send_levels(1 - mine, group)

    def finish(group):
        for number, (offset, _, _) in enumerate(plan.messages):

            @pl.when(inside(pair - offset))
            def _(group=group, number=number):
                grad_copy(group, number).wait_recv()

        for u in range(2):
            _, _, first, rows = plan.uses[1 - u][0]
            near = pair_matrix(rows, block_rows)
            for which in range(2):
                total = own[u, which, :, columns(group)]
                total = total + contract(
                    near, far_grad[1 - u, which, pl.ds(first, rows), columns(group)], 0, 0
                )
                total = total + contract(
                    spread[u], grecv[which, :, columns(group)], 0, 0
                )
                total_s[u, which, :, columns(group)] = total.astype(BF16)
        for which in (1, 2):
            result_copy(which, group).start()
            result_own(which, group).start()

    barrier = pltpu.get_barrier_semaphore()
    greeted = crew - 1
    for step in range(1, crew):
        part, other = seat(step)
        pl.semaphore_signal(
            barrier, inc=1,
            device_id={"seq": 2 * pair + part, "head": other}, device_id_type=MESH,
        )
    for distance in range(1, plan.reach + 1):
        for offset in (distance, -distance):
            valid = inside(pair + offset)
            greeted = greeted + valid.astype(jnp.int32)

            @pl.when(valid)
            def _(offset=offset):
                pl.semaphore_signal(
                    barrier, inc=1, device_id=rail(pair + offset), device_id_type=MESH
                )

    for which in range(3):
        for group in range(GROUPS):
            own_copy(which, group).start()
    for chunk in range(chunks):
        cot_own(chunk).start()

    pl.semaphore_wait(barrier, greeted)
    send_near(0)
    send_own(0)
    send_rest(0)
    send_near(1)
    send_own(1)
    send_mate(0)
    send_rest(1)

    for t in range(2):
        bias[t, own_rows, :] = jnp.zeros((block_rows, block_rows), F32)
        for number, level, first, rows in plan.uses[t]:
            row = lax.broadcasted_iota(jnp.int32, (rows, block_rows), 0)
            shown = float(level)
            if number is not None:
                valid = inside(pair + entries[number][0])
                shown = jnp.where(valid, shown, MASKED).astype(F32)

                @pl.when(jnp.logical_not(valid))
                def _(t=t, first=first, rows=rows):
                    keyset[t, :, pl.ds(block_rows + first, rows), :] = jnp.zeros(
                        (2, rows, half), BF16
                    )

            bias[t, pl.ds(block_rows + first, rows), :] = jnp.where(
                row < (block_rows >> level), shown, MASKED
            )
        for number, (_, part, level, rows) in enumerate(entries):
            row = lax.broadcasted_iota(jnp.int32, (rows, block_rows), 0)
            col = lax.broadcasted_iota(jnp.int32, (rows, block_rows), 1)
            taken = (col >> level) == (row if part == t else -1)
            spread[t, pl.ds(plan.first[number], rows), :] = jnp.where(
                taken, 0.5**level, 0.0
            ).astype(BF16)

    for offset, first, rows in plan.messages:

        @pl.when(jnp.logical_not(inside(pair - offset)))
        def _(first=first, rows=rows):
            grecv[:, pl.ds(first, rows), :] = jnp.zeros((2, rows, half), BF16)

    send_mate(1)
    for group in range(GROUPS):
        if group + 2 < GROUPS:
            send_near(group + 2)
            send_own(group + 2)
            send_rest(group + 2)
        own_copy(2, group).wait()
        mate_copy(2, group).wait_recv()
        if group % CHUNK == 0:
            cot_own(group // CHUNK).wait()
            for step in range(1, crew):
                cot_copy(group // CHUNK, step).wait_recv()
        for t in range(2):
            _, _, first, rows = plan.uses[t][0]
            keyset[t, :, pl.ds(block_rows + first, rows), columns(group)] = pyramid[0][
                1 - t, :, :, columns(group)
            ]
        for number, (offset, _, level, rows) in enumerate(entries):

            @pl.when(inside(pair + offset))
            def _(group=group, number=number, level=level, rows=rows):
                kv_copy(group, number).wait_recv()
                for which in range(2):
                    fine = rbuf[which, pl.ds(plan.first[number], rows), columns(group)]
                    for t in range(2):
                        for other, use_level, first, use_rows in plan.uses[t]:
                            if other == number:
                                held = fine
                                if use_level != level:
                                    held = contract(pair_matrix(use_rows, rows), fine, 1, 0)
                                keyset[
                                    t, which, pl.ds(block_rows + first, use_rows), columns(group)
                                ] = held.astype(BF16)

        if group + 2 < GROUPS:
            send_mate(group + 2)

        def head_pass(head_number, carry, group=group):
            held = pl.ds(pl.multiple_of(head_number * HEAD_DIM, HEAD_DIM), HEAD_DIM)
            cols = pl.ds(pl.multiple_of(group * span + head_number * HEAD_DIM, HEAD_DIM), HEAD_DIM)
            both = range(2)
            set_rows = [pl.ds(0, block_rows + plan.far_rows[t]) for t in both]
            query, grad = [q_s[t, :, cols] for t in both], [cot[t, :, cols] for t in both]
            key = [keyset[t, 0, set_rows[t], cols] for t in both]
            value = [keyset[t, 1, set_rows[t], cols] for t in both]
            scores = [
                contract(key[t], query[t], 1, 1) * (score_scale / LOG_TWO) + bias[t, set_rows[t], :]
                for t in both
            ]
            weight_grad = [contract(value[t], grad[t], 1, 1) for t in both]
            raised = [jnp.exp2(part - jnp.max(part, axis=0, keepdims=True)) for part in scores]
            weights = [part * (1.0 / jnp.sum(part, axis=0, keepdims=True)) for part in raised]
            weights_low = [part.astype(BF16) for part in weights]
            row_term = [
                jnp.sum(weights[t] * weight_grad[t], axis=0, keepdims=True) for t in both
            ]
            score_grad = [
                (weights[t] * ((weight_grad[t] - row_term[t]) * score_scale)).astype(BF16)
                for t in both
            ]
            for t in both:
                held_s[t, 0, set_rows[t], held] = score_grad[t]
                held_s[t, 1, set_rows[t], held] = weights_low[t]
                for which, (left, right) in enumerate(
                    ((score_grad[t], query[t]), (weights_low[t], grad[t]))
                ):
                    set_grad = contract(left, right, 1, 0)
                    own[t, which, :, cols] = set_grad[:block_rows]
                    far_grad[t, which, pl.ds(0, plan.far_rows[t]), cols] = set_grad[
                        block_rows:
                    ].astype(BF16)
            return carry

        def token_pass(head_number, carry, group=group):
            held = pl.ds(pl.multiple_of(head_number * HEAD_DIM, HEAD_DIM), HEAD_DIM)
            cols = pl.ds(pl.multiple_of(group * span + head_number * HEAD_DIM, HEAD_DIM), HEAD_DIM)
            for t in range(2):
                rows = pl.ds(0, block_rows + plan.far_rows[t])
                for which, out in enumerate((qg_s, att_s)):
                    out[t, :, cols] = contract(
                        held_s[t, which, rows, held], keyset[t, which, rows, cols], 0, 0
                    ).astype(BF16)
            return carry

        lax.fori_loop(0, span // HEAD_DIM, head_pass, 0)
        for number, (offset, _, level, rows) in enumerate(entries):

            @pl.when(inside(pair + offset))
            def _(group=group, number=number, level=level, rows=rows):
                for which in range(2):
                    summed = None
                    for t in range(2):
                        for other, use_level, first, use_rows in plan.uses[t]:
                            if other == number:
                                term = far_grad[t, which, pl.ds(first, use_rows), columns(group)]
                                if use_level != level:
                                    term = contract(pair_matrix(use_rows, rows), term, 0, 0)
                                term = term.astype(F32)
                                summed = term if summed is None else summed + term
                    gsend[which, pl.ds(plan.first[number], rows), columns(group)] = summed.astype(
                        BF16
                    )

        for number, (offset, _, _) in enumerate(plan.messages):

            @pl.when(inside(pair + offset))
            def _(group=group, number=number):
                grad_copy(group, number).start()

        lax.fori_loop(0, span // HEAD_DIM, token_pass, 0)
        if group % CHUNK == CHUNK - 1:
            for step in range(1, crew):
                att_copy(group // CHUNK, step).start()
            att_own(group // CHUNK).start()
        result_copy(0, group).start()
        result_own(0, group).start()
        if group >= 2:
            finish(group - 2)

    for group in range(GROUPS):
        for which in range(3):
            mate_copy(which, group).wait_send()
        for number, (offset, _, _, _) in enumerate(entries):

            @pl.when(inside(pair - offset))
            def _(group=group, number=number):
                kv_copy(group, number).wait_send()

    for chunk in range(chunks):
        for step in range(1, crew):
            cot_copy(chunk, step).wait_send()

    for group in range(max(0, GROUPS - 2), GROUPS):
        finish(group)

    for chunk in range(chunks):
        att_own(chunk).wait()
        for step in range(1, crew):
            att_copy(chunk, step).wait()
    for group in range(GROUPS):
        for number, (offset, _, _) in enumerate(plan.messages):

            @pl.when(inside(pair + offset))
            def _(group=group, number=number):
                grad_copy(group, number).wait_send()

        for which in range(3):
            result_own(which, group).wait()
            result_copy(which, group).wait()


def write_out(*refs):
    loads, stores = [], []
    for number in range(4):
        held = refs[8 + number]
        loads.append(pltpu.make_async_copy(refs[number], held, refs[12].at[number]))
        stores.append(pltpu.make_async_copy(held, refs[4 + number], refs[13].at[number]))
    for load in loads:
        load.start()
    for load, store in zip(loads, stores):
        load.wait()
        store.start()
    for store in stores:
        store.wait()


def local(blocks, heads_axis, queries, key_states, value_states, cotangent):
    block_rows, width = queries.shape
    plan = Plan(blocks, block_rows)
    half = width // 2
    count = len(plan.entries)
    far_rows = max(plan.far_rows)
    set_rows = block_rows + far_rows
    levels = max(entry[2] for entry in plan.entries)
    steps = 2 * heads_axis - 1
    chunks = GROUPS // CHUNK
    messages = len(plan.messages)
    dma = pltpu.SemaphoreType.DMA
    anywhere = pl.BlockSpec(memory_space=pl.ANY)
    scratch = [
        pltpu.VMEM((2, 2, set_rows, half), BF16),
        pltpu.VMEM((2, block_rows, half), BF16),
        pltpu.VMEM((2, block_rows, half), BF16),
        pltpu.VMEM((2, set_rows, block_rows), F32),
        pltpu.VMEM((2, 2, block_rows, half), F32),
        pltpu.VMEM((2, 2, far_rows, half), BF16),
        pltpu.VMEM((2, plan.entry_rows, half), BF16),
        pltpu.VMEM((2, plan.entry_rows, half), BF16),
        pltpu.VMEM((2, plan.entry_rows, half), BF16),
        pltpu.VMEM((2, plan.entry_rows, block_rows), BF16),
        pltpu.VMEM((2, 2, set_rows, half // GROUPS), BF16),
        pltpu.VMEM((2, block_rows, half), BF16),
        pltpu.VMEM((2, block_rows, half), BF16),
        pltpu.VMEM((2, 2, block_rows, half), BF16),
        [
            pltpu.VMEM((2, 2, rows_of(level, block_rows), half), BF16)
            for level in range(1, levels + 1)
        ],
        dma((3, GROUPS)),
        dma((chunks,)),
        dma((3, GROUPS)),
        dma((chunks,)),
        dma((3, GROUPS)),
        dma((3, GROUPS)),
        dma((GROUPS, count)),
        dma((GROUPS, count)),
        dma((GROUPS, messages)),
        dma((GROUPS, messages)),
        dma((chunks, steps)),
        dma((chunks, steps)),
        dma((chunks, steps)),
        dma((chunks, steps)),
        dma((3, GROUPS)),
        dma((3, GROUPS)),
    ]
    part = jax.ShapeDtypeStruct(queries.shape, BF16)
    results = pl.pallas_call(
        functools.partial(kernel, plan, heads_axis),
        out_shape=(jax.ShapeDtypeStruct(cotangent.shape, BF16), part, part, part),
        in_specs=[anywhere] * 4,
        out_specs=(anywhere,) * 4,
        scratch_shapes=scratch,
        cost_estimate=pl.CostEstimate(
            flops=12 * block_rows * set_rows * width,
            bytes_accessed=16 * block_rows * width,
            transcendentals=block_rows * set_rows * width // HEAD_DIM,
        ),
        compiler_params=pltpu.CompilerParams(
            collective_id=0, has_side_effects=True, vmem_limit_bytes=60 * 2**20
        ),
    )(queries, key_states, value_states, cotangent)
    return pl.pallas_call(
        write_out,
        out_shape=tuple(jax.ShapeDtypeStruct(part.shape, part.dtype) for part in results),
        in_specs=[anywhere] * 4,
        out_specs=(anywhere,) * 4,
        scratch_shapes=[pltpu.VMEM(part.shape, BF16) for part in results] + [dma((4,)), dma((4,))],
        compiler_params=pltpu.CompilerParams(vmem_limit_bytes=60 * 2**20),
    )(*results)


def solution(mesh):
    placed = (P("seq", "head"), P("seq", "head"), P("seq", "head"), P(("seq", "head"), None))
    return jax.shard_map(
        functools.partial(local, mesh.shape["seq"], mesh.shape["head"]),
        mesh=mesh,
        in_specs=placed,
        out_specs=(P(("seq", "head"), None), P("seq", "head"), P("seq", "head"), P("seq", "head")),
        check_vma=False,
    )
```

```python
import functools
import math

import jax
import jax.numpy as jnp
from jax import lax
from jax.experimental import pallas as pl
from jax.experimental.pallas import tpu as pltpu
from jax.sharding import PartitionSpec as P

HEAD_DIM = 128
LEVELS = 4
GROUPS = 4
CHUNK = 1

LOG_TWO = math.log(2.0)
MASKED = -1e30
MESH = pl.DeviceIdType.MESH
F32 = jnp.float32
BF16 = jnp.bfloat16


def rows_of(level, block_rows):
    return max(16, block_rows >> level)


class Plan:
    def __init__(self, blocks, block_rows):
        self.pairs = blocks // 2
        farthest = 2**LEVELS - 1
        self.reach = min((farthest + 1) // 2, self.pairs - 1)
        self.entries = []
        self.first = []
        self.uses = [[], []]
        self.far_rows = [0, 0]
        self.messages = []
        self.entry_rows = 0
        for t in range(2):
            self.use(t, None, 1, block_rows)
        for distance in range(1, self.reach + 1):
            for offset in (distance, -distance):
                start = self.entry_rows
                for part in range(2):
                    gaps = [abs(2 * offset + part - t) for t in range(2)]
                    levels = [gap.bit_length() if gap <= farthest else None for gap in gaps]
                    known = [level for level in levels if level is not None]
                    if not known:
                        continue
                    level = min(known)
                    rows = rows_of(level, block_rows)
                    number = len(self.entries)
                    self.entries.append((offset, part, level, rows))
                    self.first.append(self.entry_rows)
                    self.entry_rows += rows
                    for t in range(2):
                        if levels[t] is not None:
                            self.use(t, number, levels[t], block_rows)
                self.messages.append((offset, start, self.entry_rows - start))

    def use(self, t, number, level, block_rows):
        rows = rows_of(level, block_rows)
        self.uses[t].append((number, level, self.far_rows[t], rows))
        self.far_rows[t] += rows


def contract(left, right, left_dim, right_dim):
    return lax.dot_general(
        left, right, (((left_dim,), (right_dim,)), ((), ())), preferred_element_type=F32
    )


def pair_matrix(rows, wide):
    row = lax.broadcasted_iota(jnp.int32, (rows, wide), 0)
    col = lax.broadcasted_iota(jnp.int32, (rows, wide), 1)
    return jnp.where((col >> 1) == row, 0.5, 0.0).astype(BF16)


def kernel(
    plan, heads_axis,
    q_hbm, k_hbm, v_hbm, c_hbm,
    att_out, qg_out, kg_out, vg_out,
    keyset, q_s, cot, bias, own, far_grad, rbuf, gsend, grecv, spread, att_s, qg_s, total_s, pyramid,
    own_sem, cot_own_sem, out_own_sem, att_own_sem, send_in, recv_in, ksend, krecv,
    gsem, gland, csend, crecv, asend, arecv, send_out, recv_out,
):
    block_rows, width = q_hbm.shape
    out_rows = c_hbm.shape[0]
    half = width // 2
    span = half // GROUPS
    wide = CHUNK * span
    chunks = GROUPS // CHUNK
    entries = plan.entries
    position = lax.axis_index("seq")
    my_head = lax.axis_index("head")
    pair, mine = position // 2, position % 2
    mate = 2 * pair + 1 - mine
    crew = 2 * heads_axis
    my_seat = mine * heads_axis + my_head
    own_rows = pl.ds(0, block_rows)
    score_scale = 1.0 / math.sqrt(HEAD_DIM)

    def inside(other):
        return (other >= 0) & (other < plan.pairs)

    def rail(other):
        return {"seq": 2 * other + mine, "head": my_head}

    def seat(step):
        other = (my_seat + step) % crew
        return other // heads_axis, other % heads_axis

    def columns(group):
        return pl.ds(group * span, span)

    def side(part, group):
        return pl.ds(pl.multiple_of(part * half + group * span, 128), span)

    def remote(src, dst, send_sem, recv_sem, device):
        return pltpu.make_async_remote_copy(
            src_ref=src, dst_ref=dst, send_sem=send_sem, recv_sem=recv_sem,
            device_id=device, device_id_type=MESH,
        )

    def block_place(which, part, group):
        if which == 2:
            return q_s.at[part, :, columns(group)]
        return keyset.at[part, which, own_rows, columns(group)]

    def own_copy(which, group):
        return pltpu.make_async_copy(
            (k_hbm, v_hbm, q_hbm)[which].at[:, side(mine, group)],
            block_place(which, mine, group),
            own_sem.at[which, group],
        )

    def mate_copy(which, group):
        return remote(
            (k_hbm, v_hbm, q_hbm)[which].at[:, side(1 - mine, group)],
            block_place(which, mine, group),
            send_in.at[which, group],
            recv_in.at[which, group],
            {"seq": mate, "head": my_head},
        )

    def cot_source(part, other_head, chunk):
        first = other_head * width + part * half + chunk * wide
        return c_hbm.at[:, pl.ds(pl.multiple_of(first, 128), wide)]

    def cot_place(chunk):
        return cot.at[mine, pl.ds(pl.multiple_of(my_head * out_rows, 16), out_rows), pl.ds(chunk * wide, wide)]

    def cot_copy(chunk, step):
        part, other = seat(step)
        return remote(
            cot_source(part, other, chunk), cot_place(chunk),
            csend.at[chunk, step - 1], crecv.at[chunk, step - 1],
            {"seq": 2 * pair + part, "head": other},
        )

    def cot_own(chunk):
        return pltpu.make_async_copy(
            cot_source(mine, my_head, chunk), cot_place(chunk), cot_own_sem.at[chunk]
        )

    def att_source(part, other_head, chunk):
        return att_s.at[
            part, pl.ds(pl.multiple_of(other_head * out_rows, 16), out_rows), pl.ds(chunk * wide, wide)
        ]

    def att_place(chunk):
        first = my_head * width + mine * half + chunk * wide
        return att_out.at[:, pl.ds(pl.multiple_of(first, 128), wide)]

    def att_copy(chunk, step):
        part, other = seat(step)
        return remote(
            att_source(part, other, chunk), att_place(chunk),
            asend.at[chunk, step - 1], arecv.at[chunk, step - 1],
            {"seq": 2 * pair + part, "head": other},
        )

    def att_own(chunk):
        return pltpu.make_async_copy(
            att_source(mine, my_head, chunk), att_place(chunk), att_own_sem.at[chunk]
        )

    def kv_copy(group, number):
        offset, part, level, rows = entries[number]
        return remote(
            pyramid[level - 1].at[part, :, :, columns(group)],
            rbuf.at[:, pl.ds(plan.first[number], rows), columns(group)],
            ksend.at[group, number], krecv.at[group, number], rail(pair - offset),
        )

    def grad_copy(group, number):
        offset, first, rows = plan.messages[number]
        place = (slice(None), pl.ds(first, rows), columns(group))
        return remote(
            gsend.at[place], grecv.at[place],
            gsem.at[group, number], gland.at[group, number], rail(pair + offset),
        )

    def result(which, part, group):
        if which == 0:
            return qg_s.at[part, :, columns(group)]
        return total_s.at[part, which - 1, :, columns(group)]

    def result_own(which, group):
        return pltpu.make_async_copy(
            result(which, mine, group),
            (qg_out, kg_out, vg_out)[which].at[:, side(mine, group)],
            out_own_sem.at[which, group],
        )

    def result_copy(which, group):
        return remote(
            result(which, 1 - mine, group),
            (qg_out, kg_out, vg_out)[which].at[:, side(mine, group)],
            send_out.at[which, group], recv_out.at[which, group],
            {"seq": mate, "head": my_head},
        )

    def make_levels(part, group):
        for which in range(2):
            lower = keyset[part, which, own_rows, columns(group)]
            for level_ref in pyramid:
                pairs = pair_matrix(level_ref.shape[2], lower.shape[0])
                lower = contract(pairs, lower, 1, 0).astype(BF16)
                level_ref[part, which, :, columns(group)] = lower

    def send_levels(part, group):
        for number, entry in enumerate(entries):

            @pl.when((part == entry[1]) & inside(pair - entry[0]))
            def _(number=number):
                kv_copy(group, number).start()

    def send_near(group):
        for which in range(2):
            mate_copy(which, group).start()

    def send_own(group):
        for which in range(2):
            own_copy(which, group).wait()
        make_levels(mine, group)
        send_levels(mine, group)

    def send_rest(group):
        mate_copy(2, group).start()
        if group % CHUNK == 0:
            for step in range(1, crew):
                cot_copy(group // CHUNK, step).start()

    def send_mate(group):
        for which in range(2):
            mate_copy(which, group).wait_recv()
        make_levels(1 - mine, group)
        send_levels(1 - mine, group)

    def finish(group):
        for number, (offset, _, _) in enumerate(plan.messages):

            @pl.when(inside(pair - offset))
            def _(group=group, number=number):
                grad_copy(group, number).wait_recv()

        for u in range(2):
            _, _, first, rows = plan.uses[1 - u][0]
            near = pair_matrix(rows, block_rows)
            for which in range(2):
                total = own[u, which, :, columns(group)]
                total = total + contract(
                    near, far_grad[1 - u, which, pl.ds(first, rows), columns(group)], 0, 0
                )
                total = total + contract(
                    spread[u], grecv[which, :, columns(group)], 0, 0
                )
                total_s[u, which, :, columns(group)] = total.astype(BF16)
        for which in (1, 2):
            result_copy(which, group).start()
            result_own(which, group).start()

    barrier = pltpu.get_barrier_semaphore()
    greeted = crew - 1
    for step in range(1, crew):
        part, other = seat(step)
        pl.semaphore_signal(
            barrier, inc=1,
            device_id={"seq": 2 * pair + part, "head": other}, device_id_type=MESH,
        )
    for distance in range(1, plan.reach + 1):
        for offset in (distance, -distance):
            valid = inside(pair + offset)
            greeted = greeted + valid.astype(jnp.int32)

            @pl.when(valid)
            def _(offset=offset):
                pl.semaphore_signal(
                    barrier, inc=1, device_id=rail(pair + offset), device_id_type=MESH
                )

    for which in range(3):
        for group in range(GROUPS):
            own_copy(which, group).start()
    for chunk in range(chunks):
        cot_own(chunk).start()

    pl.semaphore_wait(barrier, greeted)
    for group in range(GROUPS):
        send_near(group)
        send_rest(group)
        if group == 0:
            send_own(0)
    for group in range(1, GROUPS):
        send_own(group)
        if group == 1:
            send_mate(0)

    for t in range(2):
        bias[t, own_rows, :] = jnp.zeros((block_rows, block_rows), F32)
        for number, level, first, rows in plan.uses[t]:
            row = lax.broadcasted_iota(jnp.int32, (rows, block_rows), 0)
            shown = float(level)
            if number is not None:
                valid = inside(pair + entries[number][0])
                shown = jnp.where(valid, shown, MASKED).astype(F32)

                @pl.when(jnp.logical_not(valid))
                def _(t=t, first=first, rows=rows):
                    keyset[t, :, pl.ds(block_rows + first, rows), :] = jnp.zeros(
                        (2, rows, half), BF16
                    )

            bias[t, pl.ds(block_rows + first, rows), :] = jnp.where(
                row < (block_rows >> level), shown, MASKED
            )
        for number, (_, part, level, rows) in enumerate(entries):
            row = lax.broadcasted_iota(jnp.int32, (rows, block_rows), 0)
            col = lax.broadcasted_iota(jnp.int32, (rows, block_rows), 1)
            taken = (col >> level) == (row if part == t else -1)
            spread[t, pl.ds(plan.first[number], rows), :] = jnp.where(
                taken, 0.5**level, 0.0
            ).astype(BF16)

    for offset, first, rows in plan.messages:

        @pl.when(jnp.logical_not(inside(pair - offset)))
        def _(first=first, rows=rows):
            grecv[:, pl.ds(first, rows), :] = jnp.zeros((2, rows, half), BF16)

    send_mate(1)
    for group in range(GROUPS):
        own_copy(2, group).wait()
        mate_copy(2, group).wait_recv()
        if group % CHUNK == 0:
            cot_own(group // CHUNK).wait()
            for step in range(1, crew):
                cot_copy(group // CHUNK, step).wait_recv()
        for t in range(2):
            _, _, first, rows = plan.uses[t][0]
            keyset[t, :, pl.ds(block_rows + first, rows), columns(group)] = pyramid[0][
                1 - t, :, :, columns(group)
            ]
        for number, (offset, _, level, rows) in enumerate(entries):

            @pl.when(inside(pair + offset))
            def _(group=group, number=number, level=level, rows=rows):
                kv_copy(group, number).wait_recv()
                for which in range(2):
                    fine = rbuf[which, pl.ds(plan.first[number], rows), columns(group)]
                    for t in range(2):
                        for other, use_level, first, use_rows in plan.uses[t]:
                            if other == number:
                                held = fine
                                if use_level != level:
                                    held = contract(pair_matrix(use_rows, rows), fine, 1, 0)
                                keyset[
                                    t, which, pl.ds(block_rows + first, use_rows), columns(group)
                                ] = held.astype(BF16)

        if group + 2 < GROUPS:
            send_mate(group + 2)

        def head_pass(head_number, carry, group=group):
            cols = pl.ds(pl.multiple_of(group * span + head_number * HEAD_DIM, HEAD_DIM), HEAD_DIM)
            both = range(2)
            set_rows = [pl.ds(0, block_rows + plan.far_rows[t]) for t in both]
            query, grad = [q_s[t, :, cols] for t in both], [cot[t, :, cols] for t in both]
            key = [keyset[t, 0, set_rows[t], cols] for t in both]
            value = [keyset[t, 1, set_rows[t], cols] for t in both]
            scores = [
                contract(key[t], query[t], 1, 1) * (score_scale / LOG_TWO) + bias[t, set_rows[t], :]
                for t in both
            ]
            weight_grad = [contract(value[t], grad[t], 1, 1) for t in both]
            raised = [jnp.exp2(part - jnp.max(part, axis=0, keepdims=True)) for part in scores]
            weights = [part * (1.0 / jnp.sum(part, axis=0, keepdims=True)) for part in raised]
            weights_low = [part.astype(BF16) for part in weights]
            row_term = [
                jnp.sum(weights[t] * weight_grad[t], axis=0, keepdims=True) for t in both
            ]
            score_grad = [
                (weights[t] * ((weight_grad[t] - row_term[t]) * score_scale)).astype(BF16)
                for t in both
            ]
            for t in both:
                att_s[t, :, cols] = contract(weights_low[t], value[t], 0, 0).astype(BF16)
                qg_s[t, :, cols] = contract(score_grad[t], key[t], 0, 0).astype(BF16)
                for which, (left, right) in enumerate(
                    ((score_grad[t], query[t]), (weights_low[t], grad[t]))
                ):
                    set_grad = contract(left, right, 1, 0)
                    own[t, which, :, cols] = set_grad[:block_rows]
                    far_grad[t, which, pl.ds(0, plan.far_rows[t]), cols] = set_grad[
                        block_rows:
                    ].astype(BF16)
            return carry

        lax.fori_loop(0, span // HEAD_DIM, head_pass, 0)
        for number, (offset, _, level, rows) in enumerate(entries):

            @pl.when(inside(pair + offset))
            def _(group=group, number=number, level=level, rows=rows):
                for which in range(2):
                    summed = None
                    for t in range(2):
                        for other, use_level, first, use_rows in plan.uses[t]:
                            if other == number:
                                term = far_grad[t, which, pl.ds(first, use_rows), columns(group)]
                                if use_level != level:
                                    term = contract(pair_matrix(use_rows, rows), term, 0, 0)
                                term = term.astype(F32)
                                summed = term if summed is None else summed + term
                    gsend[which, pl.ds(plan.first[number], rows), columns(group)] = summed.astype(
                        BF16
                    )

        for number, (offset, _, _) in enumerate(plan.messages):

            @pl.when(inside(pair + offset))
            def _(group=group, number=number):
                grad_copy(group, number).start()

        if group % CHUNK == CHUNK - 1:
            for step in range(1, crew):
                att_copy(group // CHUNK, step).start()
            att_own(group // CHUNK).start()
        result_copy(0, group).start()
        result_own(0, group).start()
        if group >= 2:
            finish(group - 2)

    for group in range(GROUPS):
        for which in range(3):
            mate_copy(which, group).wait_send()
        for number, (offset, _, _, _) in enumerate(entries):

            @pl.when(inside(pair - offset))
            def _(group=group, number=number):
                kv_copy(group, number).wait_send()

    for chunk in range(chunks):
        for step in range(1, crew):
            cot_copy(chunk, step).wait_send()

    for group in range(max(0, GROUPS - 2), GROUPS):
        finish(group)

    for chunk in range(chunks):
        att_own(chunk).wait()
        for step in range(1, crew):
            att_copy(chunk, step).wait()
    for group in range(GROUPS):
        for number, (offset, _, _) in enumerate(plan.messages):

            @pl.when(inside(pair + offset))
            def _(group=group, number=number):
                grad_copy(group, number).wait_send()

        for which in range(3):
            result_own(which, group).wait()
            result_copy(which, group).wait()


def write_out(*refs):
    loads, stores = [], []
    for number in range(4):
        held = refs[8 + number]
        loads.append(pltpu.make_async_copy(refs[number], held, refs[12].at[number]))
        stores.append(pltpu.make_async_copy(held, refs[4 + number], refs[13].at[number]))
    for load in loads:
        load.start()
    for load, store in zip(loads, stores):
        load.wait()
        store.start()
    for store in stores:
        store.wait()


def local(blocks, heads_axis, queries, key_states, value_states, cotangent):
    block_rows, width = queries.shape
    plan = Plan(blocks, block_rows)
    half = width // 2
    count = len(plan.entries)
    far_rows = max(plan.far_rows)
    set_rows = block_rows + far_rows
    levels = max(entry[2] for entry in plan.entries)
    steps = 2 * heads_axis - 1
    chunks = GROUPS // CHUNK
    messages = len(plan.messages)
    dma = pltpu.SemaphoreType.DMA
    anywhere = pl.BlockSpec(memory_space=pl.ANY)
    scratch = [
        pltpu.VMEM((2, 2, set_rows, half), BF16),
        pltpu.VMEM((2, block_rows, half), BF16),
        pltpu.VMEM((2, block_rows, half), BF16),
        pltpu.VMEM((2, set_rows, block_rows), F32),
        pltpu.VMEM((2, 2, block_rows, half), F32),
        pltpu.VMEM((2, 2, far_rows, half), BF16),
        pltpu.VMEM((2, plan.entry_rows, half), BF16),
        pltpu.VMEM((2, plan.entry_rows, half), BF16),
        pltpu.VMEM((2, plan.entry_rows, half), BF16),
        pltpu.VMEM((2, plan.entry_rows, block_rows), BF16),
        pltpu.VMEM((2, block_rows, half), BF16),
        pltpu.VMEM((2, block_rows, half), BF16),
        pltpu.VMEM((2, 2, block_rows, half), BF16),
        [
            pltpu.VMEM((2, 2, rows_of(level, block_rows), half), BF16)
            for level in range(1, levels + 1)
        ],
        dma((3, GROUPS)),
        dma((chunks,)),
        dma((3, GROUPS)),
        dma((chunks,)),
        dma((3, GROUPS)),
        dma((3, GROUPS)),
        dma((GROUPS, count)),
        dma((GROUPS, count)),
        dma((GROUPS, messages)),
        dma((GROUPS, messages)),
        dma((chunks, steps)),
        dma((chunks, steps)),
        dma((chunks, steps)),
        dma((chunks, steps)),
        dma((3, GROUPS)),
        dma((3, GROUPS)),
    ]
    part = jax.ShapeDtypeStruct(queries.shape, BF16)
    results = pl.pallas_call(
        functools.partial(kernel, plan, heads_axis),
        out_shape=(jax.ShapeDtypeStruct(cotangent.shape, BF16), part, part, part),
        in_specs=[anywhere] * 4,
        out_specs=(anywhere,) * 4,
        scratch_shapes=scratch,
        cost_estimate=pl.CostEstimate(
            flops=12 * block_rows * set_rows * width,
            bytes_accessed=16 * block_rows * width,
            transcendentals=block_rows * set_rows * width // HEAD_DIM,
        ),
        compiler_params=pltpu.CompilerParams(
            collective_id=0, has_side_effects=True, vmem_limit_bytes=60 * 2**20
        ),
    )(queries, key_states, value_states, cotangent)
    return pl.pallas_call(
        write_out,
        out_shape=tuple(jax.ShapeDtypeStruct(part.shape, part.dtype) for part in results),
        in_specs=[anywhere] * 4,
        out_specs=(anywhere,) * 4,
        scratch_shapes=[pltpu.VMEM(part.shape, BF16) for part in results] + [dma((4,)), dma((4,))],
        compiler_params=pltpu.CompilerParams(vmem_limit_bytes=60 * 2**20),
    )(*results)


def solution(mesh):
    placed = (P("seq", "head"), P("seq", "head"), P("seq", "head"), P(("seq", "head"), None))
    return jax.shard_map(
        functools.partial(local, mesh.shape["seq"], mesh.shape["head"]),
        mesh=mesh,
        in_specs=placed,
        out_specs=(P(("seq", "head"), None), P("seq", "head"), P("seq", "head"), P("seq", "head")),
        check_vma=False,
    )
```
